512 devices in a mesh: dp: 32 (over z_lo, y, core), tensor: 16 (over z_hi, x).
Axes of the slice: x: 4, y: 8, z: 8 (z_hi: 4, z_lo: 2; z = z_hi * 2 + z_lo), core: 2. Of those that a mesh axis runs over, the one named last changes fastest.
Arguments:
- inputs: bfloat16 [1024, 2560], P(('dp', 'tensor')), may hold values from -6 to 6
- curvature: float32 [1024], P(('dp', 'tensor')), may hold values from 0.25 to 4
- w_gate: bfloat16 [2560, 13824], P('dp', 'tensor'), may hold values from -0.125 to 0.125
- w_up: bfloat16 [2560, 13824], P('dp', 'tensor'), may hold values from -0.125 to 0.125
- w_down: bfloat16 [13824, 2560], P('tensor', 'dp'), may hold values from -0.0546875 to 0.0546875
- v_gate: bfloat16 [2560, 13824], P('dp', 'tensor'), may hold values from -0.125 to 0.125
- v_up: bfloat16 [2560, 13824], P('dp', 'tensor'), may hold values from -0.125 to 0.125
- v_down: bfloat16 [13824, 2560], P('tensor', 'dp'), may hold values from -0.0546875 to 0.0546875
Outputs:
- tangent_out: bfloat16 [1024, 2560], P(('dp', 'tensor'))
- prod_gate: float32 [2560, 13824], P('dp', 'tensor')
- prod_up: float32 [2560, 13824], P('dp', 'tensor')
- prod_down: float32 [13824, 2560], P('tensor', 'dp')
The draws below stay inside these ranges and needn't reach their ends.
All inputs are finite; a program needn't handle non-finite values.
Results may differ from the reference program's by a relative error of at most 0.024.
Values may be sent and summed in bfloat16 or wider, within the bound.
A program may use at most 128 MiB of HBM per device.

```python
import math
import jax
import jax.numpy as jnp
from jax import lax

D = 2560
FF = 13824
GROUP = 32
TOKENS = 1024


def shard_levels(own_key, dims, shards, least, high):
    def one(position, shards_of):
        steps = jax.random.uniform(jax.random.fold_in(jax.random.fold_in(own_key, 6), position), (shards_of,), jnp.float32, least / len(shards), high / len(shards))
        return jnp.repeat(jnp.exp(steps), dims[position] // shards_of).reshape((-1,) + (1,) * (len(dims) - position - 1))

    loudness = one(*shards[0])
    for cut in shards[1:]:
        loudness = loudness * one(*cut)
    return loudness


def noise(rng, extent, deviation, limit, shards=(), held_as=jnp.bfloat16):
    result = jax.random.normal(rng, extent, jnp.float32) * deviation
    if len(shards) > 0:
        result = shard_levels(rng, extent, shards, -0.22, 0.18) * result
    return jnp.clip(result, min=-limit, max=limit).astype(held_as)


def setup_inputs(seed: int = 0) -> dict:
    keys = jax.random.split(jax.random.key(seed), 9)
    inputs = noise(keys[0], (TOKENS, D), 1.0, 6.0, ((0, 512),))
    curvature = jnp.clip(jnp.exp(math.log(4.0) - 2.7725887 * jax.random.uniform(keys[1], (TOKENS,), jnp.float32) ** shard_levels(keys[1], (TOKENS,), ((0, 512),), -0.2, 0.2)), 0.25, 4.0)
    w_gate = noise(keys[2], (D, FF), D ** -0.5, 0.125, ((0, 32), (1, 16)))
    w_up = noise(keys[3], (D, FF), D ** -0.5, 0.125, ((0, 32), (1, 16)))
    w_down = noise(keys[4], (FF, D), FF ** -0.5, 0.0546875, ((0, 16), (1, 32)))
    v_gate = noise(keys[5], (D, FF), D ** -0.5, 0.125, ((0, 32), (1, 16)))
    v_up = noise(keys[6], (D, FF), D ** -0.5, 0.125, ((0, 32), (1, 16)))
    v_down = noise(keys[7], (FF, D), FF ** -0.5, 0.0546875, ((0, 16), (1, 32)))
    return {"inputs": inputs, "curvature": curvature, "w_gate": w_gate, "w_up": w_up, "w_down": w_down, "v_gate": v_gate, "v_up": v_up, "v_down": v_down}


def batch_pass(carry, block):
    rows, curv, w_gate, w_up, w_down, v_gate, v_up, v_down = block
    prod_gate, prod_up, prod_down = carry
    gate = jnp.dot(rows, w_gate, preferred_element_type=jnp.float32)
    up = jnp.dot(rows, w_up, preferred_element_type=jnp.float32)
    dgate = jnp.dot(rows, v_gate, preferred_element_type=jnp.float32)
    dup = jnp.dot(rows, v_up, preferred_element_type=jnp.float32)
    sig = jax.nn.sigmoid(gate)
    act = gate * sig
    slope = sig * (1.0 + gate * (1.0 - sig))
    hidden = (act * up).astype(jnp.bfloat16)
    thidden = (slope * dgate * up + act * dup).astype(jnp.bfloat16)
    tangent = jnp.dot(thidden, w_down, preferred_element_type=jnp.float32) + jnp.dot(hidden, v_down, preferred_element_type=jnp.float32)
    weighted = (curv[:, None] * tangent).astype(jnp.bfloat16)
    dhid = jnp.dot(weighted, w_down.T, preferred_element_type=jnp.float32)
    bgate = (dhid * up * slope).astype(jnp.bfloat16)
    bup = (dhid * act).astype(jnp.bfloat16)
    prod_gate = prod_gate + jnp.dot(rows.T, bgate, preferred_element_type=jnp.float32)
    prod_up = prod_up + jnp.dot(rows.T, bup, preferred_element_type=jnp.float32)
    prod_down = prod_down + jnp.dot(hidden.T, weighted, preferred_element_type=jnp.float32)
    return (prod_gate, prod_up, prod_down), tangent.astype(jnp.bfloat16)


def reference(inputs, curvature, w_gate, w_up, w_down, v_gate, v_up, v_down):
    blocks = inputs.reshape(-1, GROUP, D)
    curvs = curvature.reshape(-1, GROUP)
    init = (jnp.zeros((D, FF), jnp.float32), jnp.zeros((D, FF), jnp.float32), jnp.zeros((FF, D), jnp.float32))

    def step(carry, pair):
        return batch_pass(carry, (pair[0], pair[1], w_gate, w_up, w_down, v_gate, v_up, v_down))

    totals, tangents = lax.scan(step, init, (blocks, curvs))
    return tangents.reshape(TOKENS, D), totals[0], totals[1], totals[2]
```

```python
import functools

import jax
import jax.numpy as jnp
from jax import lax
from jax.experimental import pallas as pl
from jax.experimental.pallas import tpu as pltpu
from jax.sharding import PartitionSpec as P

MESH = pl.DeviceIdType.MESH
BF = jnp.bfloat16
F32 = jnp.float32


def dot(a, b, ca, cb):
    return lax.dot_general(a, b, (((ca,), (cb,)), ((), ())), preferred_element_type=F32)


class Link:
    def __init__(self, sems, slot, src, dst, device):
        self.copy = pltpu.make_async_remote_copy(
            src_ref=src,
            dst_ref=dst,
            send_sem=sems[0].at[slot],
            recv_sem=sems[1].at[slot],
            device_id=device,
            device_id_type=MESH,
        )
        self.copy.start()

    def arrive(self):
        self.copy.wait_recv()

    def left(self):
        self.copy.wait_send()


def kernel(
    NY, NT, D, F, KP,
    xs, wg, wu, vg, vu, wd, vd,
    to, pg, pu, pd,
    stage, xin, X, W, Pf, Pd, rs_s, rs_r, dh_s, dh_r, H, B,
    Tf, Tb, trecv, wt, osend, orecv, PF, PB, C1, zs, zr,
    send_sems, recv_sems, local_sems,
):
    K = 4 * D
    R = 2 * NY
    C = 2 * NT
    M = NT * R
    dp = lax.axis_index("dp")
    t = lax.axis_index("tensor")
    c = lax.rem(dp, 2)
    y = lax.rem(lax.div(dp, 2), NY)
    z = lax.div(dp, 2 * NY)

    def at(zz, yy, cc):
        return ((zz * NY + yy) * 2 + cc, t)

    core = at(z, y, 1 - c)
    zed = at(1 - z, y, c)

    def up_y(r):
        return lax.rem(y + r + NY, NY)

    def up_t(r):
        return lax.rem(t + r, NT)

    ypeers = [at(z, up_y(r), c) for r in range(1, NY)]
    tpeers = [(dp, up_t(r)) for r in range(1, NT)]
    left, right = at(z, up_y(-1), c), at(z, up_y(1), c)

    barrier = pltpu.get_barrier_semaphore()
    peers = [core, zed] + ypeers + tpeers
    for peer in peers:
        pl.semaphore_signal(barrier, inc=1, device_id=peer, device_id_type=MESH)

    links = []
    count = [0]

    def send(src, dst, device):
        link = Link((send_sems, recv_sems), count[0], src, dst, device)
        count[0] += 1
        links.append(link)
        return link

    def rows(q):
        return pl.ds(pl.multiple_of(q * D, 16), D)

    def chunk(j, size):
        return pl.ds(pl.multiple_of(j * size, size), size)

    row = lax.broadcasted_iota(jnp.int32, (R, KP), 0)
    lane = lax.broadcasted_iota(jnp.int32, (R, KP), 1)
    for j in range(NY):
        a = xs[j]
        a = jnp.where(row == 2 * y, a[0:1], jnp.where(row == 2 * y + 1, a[1:2], 0.0))
        hi = a.astype(BF).astype(F32)
        mid = (a - hi).astype(BF).astype(F32)
        low = a - hi - mid
        stage[j] = jnp.where(lane == K + 1, mid, jnp.where(lane == K + 2, low, hi)).astype(BF)
    pl.semaphore_wait(barrier, len(peers))

    xa = [send(stage.at[up_y(r)], xin.at[r - 1], ypeers[r - 1]) for r in range(1, NY)]

    own, other = z * 2 + c, (1 - z) * 2 + c
    mats = (wg, wu, vg, vu, wd, vd)
    locals_, from_core, from_z = [], [], []
    for k, m in enumerate(mats):
        dst = W.at[k, rows(own)]
        cp = pltpu.make_async_copy(m, dst, local_sems.at[k])
        cp.start()
        locals_.append(cp)
        from_z.append(send(m, dst, zed))
        from_core.append(send(m, dst, core))
    if KP > K:
        for k in range(6):
            W[k, K:KP, :] = jnp.zeros((KP - K, F), BF)

    x16 = stage[y].astype(F32)
    for r in range(1, NY):
        xa[r - 1].arrive()
        x16 = x16 + xin[r - 1].astype(F32)
    curv = x16[:, K : K + 1] + x16[:, K + 1 : K + 2] + x16[:, K + 2 : K + 3]
    X[chunk(t, R)] = x16.astype(BF)
    xg = [send(X.at[chunk(t, R)], X.at[chunk(t, R)], p) for p in tpeers]

    forwards = {}

    def forward(k):
        from_z[k].arrive()
        forwards[k] = send(W.at[k, rows(other)], W.at[k, rows(other)], core)

    def have(k):
        locals_[k].wait()
        from_core[k].arrive()
        forwards[k].arrive()

    forward(0)
    for link in xg:
        link.arrive()
    x = X[...]

    def reduce_scatter(n, begin, part, own_part, sendbuf, recvbuf, hops, between=None):
        got = {}
        waves = {}
        for k in range(n):
            for s in range(1, max(hops[k]) + 1):
                waves.setdefault(k + s if begin else s, []).append((k, s))
        for w in sorted(waves):
            for k, s in sorted(waves[w]):
                if s == 1 and begin:
                    begin(k)
                for side in (0, 1):
                    n_hops = hops[k][side]
                    if s > n_hops:
                        continue
                    far = n_hops - s + 1
                    j = up_y(-far) if side == 0 else up_y(far)
                    v = part(k, j)
                    if s > 1:
                        got[k, side, s - 1].arrive()
                        v = v + recvbuf[k, side, s - 2].astype(F32)
                    sendbuf[k, side, s - 1] = v.astype(BF)
                    got[k, side, s] = send(
                        sendbuf.at[k, side, s - 1], recvbuf.at[k, side, s - 1], left if side == 0 else right
                    )
            if between and w in between:
                between[w]()
        out = []
        for k in range(n):
            v = own_part(k)
            for side in (0, 1):
                if hops[k][side]:
                    got[k, side, hops[k][side]].arrive()
                    v = v + recvbuf[k, side, hops[k][side] - 1].astype(F32)
            out.append(v)
        return out

    def all_gather(n, buf, hops):
        got = {}
        for s in range(1, max(max(h) for h in hops) + 1):
            for k in range(n):
                for side in (0, 1):
                    if s > hops[k][side]:
                        continue
                    if s > 1:
                        got[k, side, s - 1].arrive()
                    origin = up_y(s - 1) if side == 0 else up_y(1 - s)
                    ref = buf.at[k, chunk(origin, C)]
                    got[k, side, s] = send(ref, ref, left if side == 0 else right)

        def finish(k):
            for side in (0, 1):
                if hops[k][side]:
                    got[k, side, hops[k][side]].arrive()

        return finish

    long, short = NY // 2, NY // 2 - 1
    both = [(long, short), (short, long)] * 2

    def begin(k):
        have(k)
        Pf[k] = dot(x, W[k], 1, 0)
        if k + 1 < 4:
            forward(k + 1)

    gate, up, dgate, dup = reduce_scatter(
        4, begin, lambda k, j: Pf[k, chunk(j, C)], lambda k: Pf[k, chunk(y, C)], rs_s, rs_r, both
    )
    sig = jax.nn.sigmoid(gate)
    act = gate * sig
    slope = sig * (1.0 + gate * (1.0 - sig))
    H[0, chunk(y, C)] = (act * up).astype(BF)
    H[1, chunk(y, C)] = (slope * dgate * up + act * dup).astype(BF)
    finish = all_gather(2, H, both)
    forward(4)
    forward(5)
    have(4)
    have(5)
    finish(0)
    tangent = dot(H[0], W[5], 1, 1)
    finish(1)
    tangent = tangent + dot(H[1], W[4], 1, 1)

    Tf[...] = tangent
    Tb[...] = tangent.astype(BF)
    tr = [send(Tb.at[chunk(up_t(r), R)], trecv.at[r - 1], tpeers[r - 1]) for r in range(1, NT)]
    total = Tf[chunk(t, R)]
    for r in range(1, NT):
        tr[r - 1].arrive()
        total = total + trecv[r - 1].astype(F32)
    wt[chunk(t, R)] = (curv * total).astype(BF)
    tw = [send(wt.at[chunk(t, R)], wt.at[chunk(t, R)], p) for p in tpeers]
    osend[...] = total.astype(BF)
    oa = [send(osend, orecv.at[r - 1], ypeers[r - 1]) for r in range(1, NY)]
    for link in tw:
        link.arrive()
    weighted = wt[...]

    Pd[...] = dot(weighted, W[4], 1, 0)
    half = C // 2

    def part_of(k, j):
        return Pd[pl.ds(pl.multiple_of(j * C + k * half, half), half)]

    stage1, stage2 = {}, {}

    def product(i, lhs, rhs):
        full = dot(lhs, rhs, 0, 0)
        PF[i] = full
        PB[i] = full.astype(BF)
        for n, zz in enumerate((1 - z, z)):
            stage1[i, n] = send(PB.at[i, rows(zz * 2 + 1 - c)], C1.at[i, n], core)

    def cross(i):
        stage1[i, 0].arrive()
        zs[i] = (PF[i, rows((1 - z) * 2 + c)] + C1[i, 0].astype(F32)).astype(BF)
        stage2[i] = send(zs.at[i], zr.at[i], zed)

    def settle(i, out):
        stage1[i, 1].arrive()
        mine = PF[i, rows(z * 2 + c)] + C1[i, 1].astype(F32)
        stage2[i].arrive()
        out[...] = mine + zr[i].astype(F32)

    def early():
        product(2, weighted, H[0])

    halves = reduce_scatter(
        2, None, part_of, lambda k: part_of(k, y), dh_s, dh_r, both, {1: early}
    )
    dhid = jnp.concatenate(halves, axis=0)
    B[0, chunk(y, C)] = (dhid * up * slope).astype(BF)
    B[1, chunk(y, C)] = (dhid * act).astype(BF)
    finish = all_gather(2, B, both)
    cross(2)

    def two_rows(v):
        v = v.astype(F32)
        return [jnp.sum(jnp.where(row == 2 * y + i, v, 0.0), axis=0, keepdims=True) for i in (0, 1)]

    for r in range(NY):
        if r:
            oa[r - 1].arrive()
        a, b = two_rows(orecv[r - 1] if r else osend[...])
        j = up_y(-r)
        to[j, 0:1, :] = a
        to[j, 1:2, :] = b
    settle(2, pd)

    finish(0)
    product(0, x, B[0])
    finish(1)
    product(1, x, B[1])
    cross(0)
    cross(1)
    settle(0, pg)
    settle(1, pu)
    for link in links:
        link.left()


def on_device(NY, NT, inputs, curvature, w_gate, w_up, w_down, v_gate, v_up, v_down):
    D, F = w_gate.shape
    K = 4 * D
    KP = -(-(K + 3) // 128) * 128
    R, C = 2 * NY, 2 * NT
    M = NT * R
    long = NY // 2
    xs = inputs.reshape(2, 2, NY, 2 * D).transpose(2, 0, 1, 3).reshape(NY, 2, K).astype(F32)
    xs = jnp.concatenate([xs, jnp.broadcast_to(curvature[None, :, None], (NY, 2, KP - K))], axis=2)
    n_links = 2 * (NY - 1) + 3 * (NT - 1) + 18 + 9 + 10 * (NY - 1)
    vmem = pl.BlockSpec(memory_space=pltpu.VMEM)
    hbm = pl.BlockSpec(memory_space=pl.ANY)
    to, pg, pu, pd = pl.pallas_call(
        functools.partial(kernel, NY, NT, D, F, KP),
        out_shape=[
            jax.ShapeDtypeStruct((NY, 2, KP), F32),
            jax.ShapeDtypeStruct((D, F), F32),
            jax.ShapeDtypeStruct((D, F), F32),
            jax.ShapeDtypeStruct((D, F), F32),
        ],
        in_specs=[vmem] + [hbm] * 6,
        out_specs=[vmem] * 4,
        scratch_shapes=[
            pltpu.VMEM((NY, R, KP), BF),
            pltpu.VMEM((NY - 1, R, KP), BF),
            pltpu.VMEM((M, KP), BF),
            pltpu.VMEM((6, KP, F), BF),
            pltpu.VMEM((4, M, F), F32),
            pltpu.VMEM((M, F), F32),
            pltpu.VMEM((4, 2, long, C, F), BF),
            pltpu.VMEM((4, 2, long, C, F), BF),
            pltpu.VMEM((2, 2, long, C // 2, F), BF),
            pltpu.VMEM((2, 2, long, C // 2, F), BF),
            pltpu.VMEM((2, M, F), BF),
            pltpu.VMEM((2, M, F), BF),
            pltpu.VMEM((M, KP), F32),
            pltpu.VMEM((M, KP), BF),
            pltpu.VMEM((max(NT - 1, 1), R, KP), BF),
            pltpu.VMEM((M, KP), BF),
            pltpu.VMEM((R, KP), BF),
            pltpu.VMEM((NY - 1, R, KP), BF),
            pltpu.VMEM((3, KP, F), F32),
            pltpu.VMEM((3, KP, F), BF),
            pltpu.VMEM((3, 2, D, F), BF),
            pltpu.VMEM((3, D, F), BF),
            pltpu.VMEM((3, D, F), BF),
            pltpu.SemaphoreType.DMA((n_links,)),
            pltpu.SemaphoreType.DMA((n_links,)),
            pltpu.SemaphoreType.DMA((6,)),
        ],
        compiler_params=pltpu.CompilerParams(
            collective_id=0, has_side_effects=True, vmem_limit_bytes=48 * 1024 * 1024
        ),
    )(xs, w_gate, w_up, v_gate, v_up, w_down.T, v_down.T)
    out = to[:, :, :K].reshape(NY, 2, 2, 2 * D).transpose(1, 2, 0, 3).reshape(2, 4 * NY * D)
    return out.astype(BF), pg, pu, pd.T


def solution(mesh):
    ndp, nt = mesh.shape["dp"], mesh.shape["tensor"]
    return jax.shard_map(
        functools.partial(on_device, ndp // 4, nt),
        mesh=mesh,
        in_specs=(
            P(("dp", "tensor"), None),
            P(("dp", "tensor")),
            P("dp", "tensor"),
            P("dp", "tensor"),
            P("tensor", "dp"),
            P("dp", "tensor"),
            P("dp", "tensor"),
            P("tensor", "dp"),
        ),
        out_specs=(
            P(("dp", "tensor"), None),
            P("dp", "tensor"),
            P("dp", "tensor"),
            P("tensor", "dp"),
        ),
        check_vma=False,
    )
```

```python
import functools

import jax
import jax.numpy as jnp
from jax import lax
from jax.experimental import pallas as pl
from jax.experimental.pallas import tpu as pltpu
from jax.sharding import PartitionSpec as P

MESH = pl.DeviceIdType.MESH
BF = jnp.bfloat16
F32 = jnp.float32


def dot(a, b, ca, cb):
    return lax.dot_general(a, b, (((ca,), (cb,)), ((), ())), preferred_element_type=F32)


class Link:
    def __init__(self, sems, slot, src, dst, device):
        self.copy = pltpu.make_async_remote_copy(
            src_ref=src,
            dst_ref=dst,
            send_sem=sems[0].at[slot],
            recv_sem=sems[1].at[slot],
            device_id=device,
            device_id_type=MESH,
        )
        self.copy.start()

    def arrive(self):
        self.copy.wait_recv()

    def left(self):
        self.copy.wait_send()


def kernel(
    NY, NT, D, F, KP,
    x_in, curv_in, wg, wu, vg, vu, wd, vd,
    to, pg, pu, pd,
    stage, xin, X, W, Pf, Pd, rs_s, rs_r, dh_s, dh_r, H, B,
    Tf, Tb, trecv, wt, osend, orecv, ot, PF, PB, C1, zs, zr,
    send_sems, recv_sems, local_sems,
):
    K = 4 * D
    R = 2 * NY
    C = 2 * NT
    M = NT * R
    NX = 4 if NT % 4 == 0 else 1
    NH = NT // NX
    dp = lax.axis_index("dp")
    t = lax.axis_index("tensor")
    c = lax.rem(dp, 2)
    y = lax.rem(lax.div(dp, 2), NY)
    z = lax.div(dp, 2 * NY)

    def at(zz, yy, cc):
        return ((zz * NY + yy) * 2 + cc, t)

    core = at(z, y, 1 - c)
    zed = at(1 - z, y, c)

    def up_y(r):
        return lax.rem(y + r + NY, NY)

    def up_t(r):
        return lax.rem(t + r, NT)

    ypeers = [at(z, up_y(r), c) for r in range(1, NY)]
    tpeers = [(dp, up_t(r)) for r in range(1, NT)]
    xq, h = lax.rem(t, NX), lax.div(t, NX)

    def up_h(r):
        return lax.rem(h + r, NH) * NX + xq

    hpeers = [(dp, up_h(r)) for r in range(1, NH)]
    xpeers = [(dp, h * NX + lax.rem(xq + r, NX)) for r in range(1, NX)]
    left, right = at(z, up_y(-1), c), at(z, up_y(1), c)

    barrier = pltpu.get_barrier_semaphore()
    peers = [core, zed] + ypeers + tpeers
    for peer in peers:
        pl.semaphore_signal(barrier, inc=1, device_id=peer, device_id_type=MESH)

    links = []
    count = [0]

    def send(src, dst, device):
        link = Link((send_sems, recv_sems), count[0], src, dst, device)
        count[0] += 1
        links.append(link)
        return link

    def rows(q):
        return pl.ds(pl.multiple_of(q * D, 16), D)

    def chunk(j, size):
        return pl.ds(pl.multiple_of(j * size, size), size)

    row = lax.broadcasted_iota(jnp.int32, (R, KP), 0)
    lane = lax.broadcasted_iota(jnp.int32, (R, KP), 1)
    raw = x_in[...].astype(F32)
    tail = lax.broadcasted_iota(jnp.int32, (2, KP - K), 0)
    tail = jnp.where(tail == 0, curv_in[0], curv_in[1])
    for j in range(NY):
        parts = [raw[:, (zz * NY + j) * 2 * D : (zz * NY + j + 1) * 2 * D] for zz in (0, 1)]
        a = jnp.concatenate(parts + [tail], axis=1)
        a = jnp.where(row == 2 * y, a[0:1], jnp.where(row == 2 * y + 1, a[1:2], 0.0))
        hi = a.astype(BF).astype(F32)
        mid = (a - hi).astype(BF).astype(F32)
        low = a - hi - mid
        stage[j] = jnp.where(lane == K + 1, mid, jnp.where(lane == K + 2, low, hi)).astype(BF)
    pl.semaphore_wait(barrier, len(peers))

    xa = [send(stage.at[up_y(r)], xin.at[r - 1], ypeers[r - 1]) for r in range(1, NY)]

    own, other = z * 2 + c, (1 - z) * 2 + c
    mats = (wg, wu, vg, vu, wd, vd)
    locals_, from_core, from_z, forwards = {}, {}, {}, {}

    def fetch(k):
        dst = W.at[k, rows(own)]
        from_z[k] = send(mats[k], dst, zed)
        from_core[k] = send(mats[k], dst, core)
        locals_[k] = pltpu.make_async_copy(mats[k], dst, local_sems.at[k])
        locals_[k].start()

    def forward(k):
        from_z[k].arrive()
        forwards[k] = send(W.at[k, rows(other)], W.at[k, rows(other)], core)

    def have(k):
        locals_[k].wait()
        from_core[k].arrive()
        forwards[k].arrive()

    fetch(0)
    fetch(1)
    if KP > K:
        for k in range(6):
            W[k, K:KP, :] = jnp.zeros((KP - K, F), BF)

    x16 = stage[y].astype(F32)
    for r in range(1, NY):
        xa[r - 1].arrive()
        x16 = x16 + xin[r - 1].astype(F32)
    curv = x16[:, K : K + 1] + x16[:, K + 1 : K + 2] + x16[:, K + 2 : K + 3]
    X[chunk(t, R)] = x16.astype(BF)

    def all_tensor(buf):
        got = [send(buf.at[chunk(t, R)], buf.at[chunk(t, R)], p) for p in hpeers]

        def second():
            block = {}
            mine = [buf.at[chunk(t, R)]] + [buf.at[chunk(up_h(r), R)] for r in range(1, NH)]
            for n, ref in enumerate(mine):
                if n:
                    got[NH - 1 - n].arrive()
                for p in xpeers:
                    block[n, len(block)] = send(ref, ref, p)
            return list(block.values())

        return second

    second = all_tensor(X)
    fetch(2)
    xg = second()
    fetch(3)
    forward(0)
    forward(1)
    for link in xg:
        link.arrive()
    x = X[...]

    def reduce_scatter(n, begin, part, own_part, sendbuf, recvbuf, hops, skew, between=None):
        got = {}
        waves = {}
        for k in range(n):
            for s in range(1, max(hops[k]) + 1):
                waves.setdefault(skew[k] + s, []).append((k, s))
        for w in sorted(waves):
            for k, s in sorted(waves[w]):
                if s == 1 and begin:
                    begin(k)
                for side in (0, 1):
                    n_hops = hops[k][side]
                    if s > n_hops:
                        continue
                    far = n_hops - s + 1
                    j = up_y(-far) if side == 0 else up_y(far)
                    v = part(k, j)
                    if s > 1:
                        got[k, side, s - 1].arrive()
                        v = v + recvbuf[k, side, s - 2].astype(F32)
                    sendbuf[k, side, s - 1] = v.astype(BF)
                    got[k, side, s] = send(
                        sendbuf.at[k, side, s - 1], recvbuf.at[k, side, s - 1], left if side == 0 else right
                    )
            if between and w in between:
                between[w]()
        out = []
        for k in range(n):
            v = own_part(k)
            for side in (0, 1):
                if hops[k][side]:
                    got[k, side, hops[k][side]].arrive()
                    v = v + recvbuf[k, side, hops[k][side] - 1].astype(F32)
            out.append(v)
        return out

    def all_gather(n, buf, hops):
        got = {}
        for s in range(1, max(max(h) for h in hops) + 1):
            for k in range(n):
                for side in (0, 1):
                    if s > hops[k][side]:
                        continue
                    if s > 1:
                        got[k, side, s - 1].arrive()
                    origin = up_y(s - 1) if side == 0 else up_y(1 - s)
                    ref = buf.at[k, chunk(origin, C)]
                    got[k, side, s] = send(ref, ref, left if side == 0 else right)

        def finish(k):
            for side in (0, 1):
                if hops[k][side]:
                    got[k, side, hops[k][side]].arrive()

        return finish

    long, short = NY // 2, NY // 2 - 1
    both = [(long, short), (short, long)] * 2

    def begin(k):
        have(k)
        Pf[k] = dot(x, W[k], 1, 0)
        if k in (1, 2):
            forward(k + 1)

    gate, up, dgate, dup = reduce_scatter(
        4, begin, lambda k, j: Pf[k, chunk(j, C)], lambda k: Pf[k, chunk(y, C)], rs_s, rs_r, both, (0, 0, 1, 2),
        {3: lambda: fetch(4), 4: lambda: fetch(5)},
    )
    sig = jax.nn.sigmoid(gate)
    act = gate * sig
    slope = sig * (1.0 + gate * (1.0 - sig))
    H[0, chunk(y, C)] = (act * up).astype(BF)
    H[1, chunk(y, C)] = (slope * dgate * up + act * dup).astype(BF)
    finish = all_gather(2, H, both)
    forward(4)
    forward(5)
    have(4)
    have(5)
    finish(0)
    tangent = dot(H[0], W[5], 1, 1)
    finish(1)
    tangent = tangent + dot(H[1], W[4], 1, 1)

    Tf[...] = tangent
    Tb[...] = tangent.astype(BF)
    tr = [send(Tb.at[chunk(up_t(r), R)], trecv.at[r - 1], tpeers[r - 1]) for r in range(1, NT)]
    total = Tf[chunk(t, R)]
    for r in range(1, NT):
        tr[r - 1].arrive()
        total = total + trecv[r - 1].astype(F32)
    wt[chunk(t, R)] = (curv * total).astype(BF)
    tw = [send(wt.at[chunk(t, R)], wt.at[chunk(t, R)], p) for p in tpeers]
    osend[...] = total.astype(BF)
    oa = [send(osend, orecv.at[r - 1], ypeers[r - 1]) for r in range(1, NY)]
    for link in tw:
        link.arrive()
    weighted = wt[...]

    Pd[...] = dot(weighted, W[4], 1, 0)
    half = C // 2

    def part_of(k, j):
        return Pd[pl.ds(pl.multiple_of(j * C + k * half, half), half)]

    stage1, stage2 = {}, {}

    def product(i, lhs, rhs):
        full = dot(lhs, rhs, 0, 0)
        PF[i] = full
        PB[i] = full.astype(BF)
        for n, zz in enumerate((1 - z, z)):
            stage1[i, n] = send(PB.at[i, rows(zz * 2 + 1 - c)], C1.at[i, n], core)

    def cross(i):
        stage1[i, 0].arrive()
        zs[i] = (PF[i, rows((1 - z) * 2 + c)] + C1[i, 0].astype(F32)).astype(BF)
        stage2[i] = send(zs.at[i], zr.at[i], zed)

    def settle(i, out):
        stage1[i, 1].arrive()
        mine = PF[i, rows(z * 2 + c)] + C1[i, 1].astype(F32)
        stage2[i].arrive()
        out[...] = mine + zr[i].astype(F32)

    def early():
        product(2, weighted, H[0])

    halves = reduce_scatter(
        2, None, part_of, lambda k: part_of(k, y), dh_s, dh_r, both, (0, 0), {1: early}
    )
    dhid = jnp.concatenate(halves, axis=0)
    B[0, chunk(y, C)] = (dhid * up * slope).astype(BF)
    B[1, chunk(y, C)] = (dhid * act).astype(BF)
    finish = all_gather(2, B, both)
    cross(2)

    def two_rows(v):
        v = v.astype(F32)
        return [jnp.sum(jnp.where(row == 2 * y + i, v, 0.0), axis=0, keepdims=True) for i in (0, 1)]

    for r in range(NY):
        if r:
            oa[r - 1].arrive()
        a, b = two_rows(orecv[r - 1] if r else osend[...])
        ot[up_y(-r)] = jnp.concatenate([a, b], axis=0)
    for j in range(NY):
        v = ot[j].astype(BF)
        for zz in (0, 1):
            to[:, (zz * NY + j) * 2 * D : (zz * NY + j + 1) * 2 * D] = v[:, zz * 2 * D : (zz + 1) * 2 * D]
    settle(2, pd)

    finish(0)
    product(0, x, B[0])
    finish(1)
    product(1, x, B[1])
    cross(0)
    cross(1)
    settle(0, pg)
    settle(1, pu)
    for link in links:
        link.left()


def on_device(NY, NT, inputs, curvature, w_gate, w_up, w_down, v_gate, v_up, v_down):
    D, F = w_gate.shape
    K = 4 * D
    KP = -(-(K + 3) // 128) * 128
    R, C = 2 * NY, 2 * NT
    M = NT * R
    long = NY // 2
    n_links = 2 * (NY - 1) + 3 * (NT - 1) + 18 + 9 + 10 * (NY - 1)
    vmem = pl.BlockSpec(memory_space=pltpu.VMEM)
    hbm = pl.BlockSpec(memory_space=pl.ANY)
    to, pg, pu, pd = pl.pallas_call(
        functools.partial(kernel, NY, NT, D, F, KP),
        out_shape=[
            jax.ShapeDtypeStruct((2, 4 * NY * D), BF),
            jax.ShapeDtypeStruct((D, F), F32),
            jax.ShapeDtypeStruct((D, F), F32),
            jax.ShapeDtypeStruct((D, F), F32),
        ],
        in_specs=[vmem, pl.BlockSpec(memory_space=pltpu.SMEM)] + [hbm] * 6,
        out_specs=[vmem] * 4,
        scratch_shapes=[
            pltpu.VMEM((NY, R, KP), BF),
            pltpu.VMEM((NY - 1, R, KP), BF),
            pltpu.VMEM((M, KP), BF),
            pltpu.VMEM((6, KP, F), BF),
            pltpu.VMEM((4, M, F), F32),
            pltpu.VMEM((M, F), F32),
            pltpu.VMEM((4, 2, long, C, F), BF),
            pltpu.VMEM((4, 2, long, C, F), BF),
            pltpu.VMEM((2, 2, long, C // 2, F), BF),
            pltpu.VMEM((2, 2, long, C // 2, F), BF),
            pltpu.VMEM((2, M, F), BF),
            pltpu.VMEM((2, M, F), BF),
            pltpu.VMEM((M, KP), F32),
            pltpu.VMEM((M, KP), BF),
            pltpu.VMEM((max(NT - 1, 1), R, KP), BF),
            pltpu.VMEM((M, KP), BF),
            pltpu.VMEM((R, KP), BF),
            pltpu.VMEM((NY - 1, R, KP), BF),
            pltpu.VMEM((NY, 2, KP), F32),
            pltpu.VMEM((3, KP, F), F32),
            pltpu.VMEM((3, KP, F), BF),
            pltpu.VMEM((3, 2, D, F), BF),
            pltpu.VMEM((3, D, F), BF),
            pltpu.VMEM((3, D, F), BF),
            pltpu.SemaphoreType.DMA((n_links,)),
            pltpu.SemaphoreType.DMA((n_links,)),
            pltpu.SemaphoreType.DMA((6,)),
        ],
        compiler_params=pltpu.CompilerParams(
            collective_id=0, has_side_effects=True, vmem_limit_bytes=62 * 1024 * 1024
        ),
    )(inputs, curvature, w_gate, w_up, v_gate, v_up, w_down.T, v_down.T)
    return to, pg, pu, pd.T


def solution(mesh):
    ndp, nt = mesh.shape["dp"], mesh.shape["tensor"]
    return jax.shard_map(
        functools.partial(on_device, ndp // 4, nt),
        mesh=mesh,
        in_specs=(
            P(("dp", "tensor"), None),
            P(("dp", "tensor")),
            P("dp", "tensor"),
            P("dp", "tensor"),
            P("tensor", "dp"),
            P("dp", "tensor"),
            P("dp", "tensor"),
            P("tensor", "dp"),
        ),
        out_specs=(
            P(("dp", "tensor"), None),
            P("dp", "tensor"),
            P("dp", "tensor"),
            P("tensor", "dp"),
        ),
        check_vma=False,
    )
```

```python
import functools

import jax
import jax.numpy as jnp
from jax import lax
from jax.experimental import pallas as pl
from jax.experimental.pallas import tpu as pltpu
from jax.sharding import PartitionSpec as P

MESH = pl.DeviceIdType.MESH
BF = jnp.bfloat16
F32 = jnp.float32


def dot(a, b, ca, cb):
    return lax.dot_general(a, b, (((ca,), (cb,)), ((), ())), preferred_element_type=F32)


class Link:
    def __init__(self, sems, slot, src, dst, device):
        self.copy = pltpu.make_async_remote_copy(
            src_ref=src,
            dst_ref=dst,
            send_sem=sems[0].at[slot],
            recv_sem=sems[1].at[slot],
            device_id=device,
            device_id_type=MESH,
        )
        self.copy.start()

    def arrive(self):
        self.copy.wait_recv()

    def left(self):
        self.copy.wait_send()


def kernel(
    NY, NT, D, F, KP,
    x_in, curv_in, wg, wu, vg, vu, wd, vd,
    to, pg, pu, pd,
    stage, xin, X, W, Pf, Pd, rs_s, rs_r, dh_s, dh_r, H, A, G,
    Tf, Tb, trecv, wt, osend, orecv, ot, PF, PB, C1, zs, zr,
    send_sems, recv_sems, local_sems,
):
    K = 4 * D
    R = 2 * NY
    C = 2 * NT
    M = NT * R
    NX = 4 if NT % 4 == 0 else 1
    NH = NT // NX
    dp = lax.axis_index("dp")
    t = lax.axis_index("tensor")
    c = lax.rem(dp, 2)
    y = lax.rem(lax.div(dp, 2), NY)
    z = lax.div(dp, 2 * NY)

    def at(zz, yy, cc):
        return ((zz * NY + yy) * 2 + cc, t)

    core = at(z, y, 1 - c)
    zed = at(1 - z, y, c)

    def up_y(r):
        return lax.rem(y + r + NY, NY)

    def up_t(r):
        return lax.rem(t + r, NT)

    ypeers = [at(z, up_y(r), c) for r in range(1, NY)]
    tpeers = [(dp, up_t(r)) for r in range(1, NT)]
    xq, h = lax.rem(t, NX), lax.div(t, NX)

    def up_h(r):
        return lax.rem(h + r, NH) * NX + xq

    hpeers = [(dp, up_h(r)) for r in range(1, NH)]
    xpeers = [(dp, h * NX + lax.rem(xq + r, NX)) for r in range(1, NX)]

    barrier = pltpu.get_barrier_semaphore()
    peers = [core, zed] + ypeers + tpeers
    for peer in peers:
        pl.semaphore_signal(barrier, inc=1, device_id=peer, device_id_type=MESH)

    links = []
    count = [0]

    def send(src, dst, device):
        link = Link((send_sems, recv_sems), count[0], src, dst, device)
        count[0] += 1
        links.append(link)
        return link

    def rows(q):
        return pl.ds(pl.multiple_of(q * D, 16), D)

    def chunk(j, size):
        return pl.ds(pl.multiple_of(j * size, size), size)

    row = lax.broadcasted_iota(jnp.int32, (R, KP), 0)
    lane = lax.broadcasted_iota(jnp.int32, (R, KP), 1)
    raw = x_in[...].astype(F32)
    tail = lax.broadcasted_iota(jnp.int32, (2, KP - K), 0)
    tail = jnp.where(tail == 0, curv_in[0], curv_in[1])
    for j in range(NY):
        parts = [raw[:, (zz * NY + j) * 2 * D : (zz * NY + j + 1) * 2 * D] for zz in (0, 1)]
        a = jnp.concatenate(parts + [tail], axis=1)
        a = jnp.where(row == 2 * y, a[0:1], jnp.where(row == 2 * y + 1, a[1:2], 0.0))
        hi = a.astype(BF).astype(F32)
        mid = (a - hi).astype(BF).astype(F32)
        low = a - hi - mid
        stage[j] = jnp.where(lane == K + 1, mid, jnp.where(lane == K + 2, low, hi)).astype(BF)
    pl.semaphore_wait(barrier, len(peers))

    xa = [send(stage.at[up_y(r)], xin.at[r - 1], ypeers[r - 1]) for r in range(1, NY)]

    own, other = z * 2 + c, (1 - z) * 2 + c
    mats = (wg, wu, vg, vu, wd, vd)
    locals_, from_core, from_z, forwards = {}, {}, {}, {}

    def fetch(k):
        dst = W.at[k, rows(own)]
        from_z[k] = send(mats[k], dst, zed)
        from_core[k] = send(mats[k], dst, core)
        locals_[k] = pltpu.make_async_copy(mats[k], dst, local_sems.at[k])
        locals_[k].start()

    def forward(k):
        from_z[k].arrive()
        forwards[k] = send(W.at[k, rows(other)], W.at[k, rows(other)], core)

    def have(k):
        locals_[k].wait()
        from_core[k].arrive()
        forwards[k].arrive()

    fetch(0)
    fetch(1)
    if KP > K:
        for k in range(6):
            W[k, K:KP, :] = jnp.zeros((KP - K, F), BF)

    x16 = stage[y].astype(F32)
    for r in range(1, NY):
        xa[r - 1].arrive()
        x16 = x16 + xin[r - 1].astype(F32)
    curv = x16[:, K : K + 1] + x16[:, K + 1 : K + 2] + x16[:, K + 2 : K + 3]
    X[chunk(t, R)] = x16.astype(BF)

    def all_tensor(buf):
        got = [send(buf.at[chunk(t, R)], buf.at[chunk(t, R)], p) for p in hpeers]

        def second():
            block = {}
            mine = [buf.at[chunk(t, R)]] + [buf.at[chunk(up_h(r), R)] for r in range(1, NH)]
            for n, ref in enumerate(mine):
                if n:
                    got[NH - 1 - n].arrive()
                for p in xpeers:
                    block[n, len(block)] = send(ref, ref, p)
            return list(block.values())

        return second

    second = all_tensor(X)
    fetch(2)
    xg = second()
    fetch(3)
    forward(0)
    forward(1)
    for link in xg:
        link.arrive()
    x = X[...]

    def dist(d, n):
        return at(z, up_y(d * n), c)

    def reach(k, d):
        return NY // 2 - (1 if (k % 2 == 0) == (d > 0) else 0)

    def reduce_ring(k, part, sent, recv):
        got = {}

        def step(s):
            for i, d in enumerate((-1, 1)):
                n = reach(k, d)
                if s > n:
                    continue
                v = part(k, up_y(d * (n - s + 1)))
                if s > 1:
                    got[i].arrive()
                    v = v + recv[k, i, s - 2].astype(F32)
                sent[k, i, s - 1] = v.astype(BF)
                got[i] = send(sent.at[k, i, s - 1], recv.at[k, i, s - 1], dist(d, 1))

        def total():
            v = part(k, y)
            for i, d in enumerate((-1, 1)):
                if reach(k, d):
                    got[i].arrive()
                    v = v + recv[k, i, reach(k, d) - 1].astype(F32)
            return v

        return {s: functools.partial(step, s) for s in range(1, NY // 2 + 1)}, total

    def reduce_tree(k, part, sent, recv):
        got = {}

        def push(i, d, slot, v, far):
            sent[k, i, slot] = v.astype(BF)
            got[i, slot] = send(sent.at[k, i, slot], recv.at[k, i, slot], dist(d, far))

        def first():
            for i, d in enumerate((-1, 1)):
                if reach(k, d) == 4:
                    push(i, d, 0, part(k, up_y(4 * d)), 2)
                push(i, d, 1, part(k, up_y(3 * d)), 1)
            for i, d in enumerate((-1, 1)):
                push(i, d, 2, part(k, up_y(d)), 1)

        def second():
            for i, d in enumerate((-1, 1)):
                v = part(k, up_y(2 * d))
                for slot in (1, 0) if reach(k, d) == 4 else (1,):
                    got[i, slot].arrive()
                    v = v + recv[k, i, slot].astype(F32)
                push(i, d, 3, v, 2)

        def total():
            v = part(k, y)
            for slot in (2, 3):
                for i in (0, 1):
                    got[i, slot].arrive()
                    v = v + recv[k, i, slot].astype(F32)
            return v

        return {1: first, 2: second}, total

    def gather_ring(k, ref):
        got = {}

        def step(s):
            for i, d in enumerate((-1, 1)):
                if s > reach(k, d):
                    continue
                if s > 1:
                    got[i].arrive()
                block = ref(up_y(-d * (s - 1)))
                got[i] = send(block, block, dist(d, 1))

        def finish():
            for i in got:
                got[i].arrive()

        return {s: functools.partial(step, s) for s in range(1, NY // 2 + 1)}, finish

    def gather_tree(k, ref):
        got = {}

        def first():
            for far in (2, 1):
                for i, d in enumerate((-1, 1)):
                    got[i, 2 - far] = send(ref(y), ref(y), dist(d, far))

        def second():
            for i, d in enumerate((-1, 1)):
                got[i, 0].arrive()
                block = ref(up_y(-2 * d))
                if reach(k, d) == 4:
                    got[i, 3] = send(block, block, dist(d, 2))
                got[i, 2] = send(block, block, dist(d, 1))

        def finish():
            for i, slot in got:
                if slot:
                    got[i, slot].arrive()

        return {1: first, 2: second}, finish

    def in_waves(plans, late=None, between=None):
        steps = []
        for n, (waves, _) in enumerate(plans):
            steps += [(w + (late[n] if late else 0), n, f) for w, f in waves.items()]
        last = None
        for w, n, f in sorted(steps, key=lambda e: e[:2]):
            if between and last is not None and w != last and last in between:
                between[last]()
            last = w
            f()

    if NY != 8:
        reduce_tree, gather_tree = reduce_ring, gather_ring

    def part(k, j):
        return Pf[k, chunk(j, C)]

    def begin(k):
        have(k)
        Pf[k] = dot(x, W[k], 1, 0)
        if k in (1, 2):
            forward(k + 1)

    plans = []
    for k in range(4):
        waves, total = reduce_ring(k, part, rs_s, rs_r)

        def opened(k=k, step=waves[1]):
            begin(k)
            step()

        waves[1] = opened
        plans.append((waves, total))

    def down():
        fetch(4)
        fetch(5)

    in_waves(plans, (0, 0, 1, 2), {2: down})
    gate, up, dgate, dup = [total() for _, total in plans]
    sig = jax.nn.sigmoid(gate)
    act = gate * sig
    slope = sig * (1.0 + gate * (1.0 - sig))
    up_slope = up * slope
    H[0, chunk(y, C)] = (act * up).astype(BF)
    H[1, chunk(y, C)] = (up_slope * dgate + act * dup).astype(BF)
    A[0, chunk(y, C)] = act.astype(BF)
    A[1, chunk(y, C)] = up_slope.astype(BF)
    half = C // 2

    def piece(buf, n, q):
        return lambda j: buf.at[n, pl.ds(pl.multiple_of(j * C + q * half, half), half)]

    plans = [gather_ring(q, piece(H, n, q)) for n in (0, 1) for q in (0, 1)]
    in_waves(plans)
    forward(4)
    forward(5)
    have(4)
    have(5)
    plans[0][1]()
    plans[1][1]()
    tangent = dot(H[0], W[5], 1, 1)
    plans[2][1]()
    plans[3][1]()
    tangent = tangent + dot(H[1], W[4], 1, 1)

    Tf[...] = tangent
    Tb[...] = tangent.astype(BF)
    tr = [send(Tb.at[chunk(up_t(r), R)], trecv.at[r - 1], tpeers[r - 1]) for r in range(1, NT)]
    aplans = [gather_ring(n, lambda j, n=n: A.at[n, chunk(j, C)]) for n in (0, 1)]
    aplans[0][0][1]()
    aplans[1][0][1]()
    total = Tf[chunk(t, R)]
    for r in range(1, NT):
        tr[r - 1].arrive()
        total = total + trecv[r - 1].astype(F32)
    wt[chunk(t, R)] = (curv * total).astype(BF)
    tw = [send(wt.at[chunk(t, R)], wt.at[chunk(t, R)], p) for p in tpeers]
    osend[...] = total.astype(BF)
    oa = [send(osend, orecv.at[r - 1], ypeers[r - 1]) for r in range(1, NY)]
    for w in range(2, NY // 2 + 1):
        aplans[0][0][w]()
        aplans[1][0][w]()
    for link in tw:
        link.arrive()
    weighted = wt[...]

    Pd[...] = dot(weighted, W[4], 1, 0)

    def part_of(k, j):
        return Pd[pl.ds(pl.multiple_of(j * C + k * half, half), half)]

    stage1, stage2 = {}, {}

    def product(i, lhs, rhs):
        full = dot(lhs, rhs, 0, 0)
        PF[i] = full
        PB[i] = full.astype(BF)
        for n, zz in enumerate((1 - z, z)):
            stage1[i, n] = send(PB.at[i, rows(zz * 2 + 1 - c)], C1.at[i, n], core)

    def cross(i):
        stage1[i, 0].arrive()
        zs[i] = (PF[i, rows((1 - z) * 2 + c)] + C1[i, 0].astype(F32)).astype(BF)
        stage2[i] = send(zs.at[i], zr.at[i], zed)

    def settle(i, out):
        stage1[i, 1].arrive()
        mine = PF[i, rows(z * 2 + c)] + C1[i, 1].astype(F32)
        stage2[i].arrive()
        out[...] = mine + zr[i].astype(F32)

    plans = [reduce_tree(k, part_of, dh_s, dh_r) for k in (0, 1)]
    in_waves(plans, None, {1: lambda: product(2, weighted, H[0])} if NY == 8 else None)
    for k, (_, total) in enumerate(plans):
        G[pl.ds(pl.multiple_of(y * C + k * half, half), half)] = total().astype(BF)
    if NY != 8:
        product(2, weighted, H[0])
    plans = [gather_tree(k, lambda j, k=k: G.at[pl.ds(pl.multiple_of(j * C + k * half, half), half)]) for k in (0, 1)]
    in_waves(plans)
    for _, finish in aplans:
        finish()
    cross(2)

    def two_rows(v):
        v = v.astype(F32)
        return [jnp.sum(jnp.where(row == 2 * y + i, v, 0.0), axis=0, keepdims=True) for i in (0, 1)]

    for r in range(NY):
        if r:
            oa[r - 1].arrive()
        a, b = two_rows(orecv[r - 1] if r else osend[...])
        ot[up_y(-r)] = jnp.concatenate([a, b], axis=0)
    for j in range(NY):
        v = ot[j].astype(BF)
        for zz in (0, 1):
            to[:, (zz * NY + j) * 2 * D : (zz * NY + j + 1) * 2 * D] = v[:, zz * 2 * D : (zz + 1) * 2 * D]
    settle(2, pd)

    for _, finish in plans:
        finish()
    dhid = G[...].astype(F32)
    product(0, x, (dhid * A[1].astype(F32)).astype(BF))
    product(1, x, (dhid * A[0].astype(F32)).astype(BF))
    cross(0)
    cross(1)
    settle(0, pg)
    settle(1, pu)
    for link in links:
        link.left()


def on_device(NY, NT, inputs, curvature, w_gate, w_up, w_down, v_gate, v_up, v_down):
    D, F = w_gate.shape
    K = 4 * D
    KP = -(-(K + 3) // 128) * 128
    R, C = 2 * NY, 2 * NT
    M = NT * R
    steps = NY // 2
    n_links = 2 * (NY - 1) + 3 * (NT - 1) + 18 + 9 + 14 * (NY - 1)
    vmem = pl.BlockSpec(memory_space=pltpu.VMEM)
    hbm = pl.BlockSpec(memory_space=pl.ANY)
    to, pg, pu, pd = pl.pallas_call(
        functools.partial(kernel, NY, NT, D, F, KP),
        out_shape=[
            jax.ShapeDtypeStruct((2, 4 * NY * D), BF),
            jax.ShapeDtypeStruct((D, F), F32),
            jax.ShapeDtypeStruct((D, F), F32),
            jax.ShapeDtypeStruct((D, F), F32),
        ],
        in_specs=[vmem, pl.BlockSpec(memory_space=pltpu.SMEM)] + [hbm] * 6,
        out_specs=[vmem] * 4,
        scratch_shapes=[
            pltpu.VMEM((NY, R, KP), BF),
            pltpu.VMEM((NY - 1, R, KP), BF),
            pltpu.VMEM((M, KP), BF),
            pltpu.VMEM((6, KP, F), BF),
            pltpu.VMEM((4, M, F), F32),
            pltpu.VMEM((M, F), F32),
            pltpu.VMEM((4, 2, steps, C, F), BF),
            pltpu.VMEM((4, 2, steps, C, F), BF),
            pltpu.VMEM((2, 2, steps, C // 2, F), BF),
            pltpu.VMEM((2, 2, steps, C // 2, F), BF),
            pltpu.VMEM((2, M, F), BF),
            pltpu.VMEM((2, M, F), BF),
            pltpu.VMEM((M, F), BF),
            pltpu.VMEM((M, KP), F32),
            pltpu.VMEM((M, KP), BF),
            pltpu.VMEM((max(NT - 1, 1), R, KP), BF),
            pltpu.VMEM((M, KP), BF),
            pltpu.VMEM((R, KP), BF),
            pltpu.VMEM((NY - 1, R, KP), BF),
            pltpu.VMEM((NY, 2, KP), F32),
            pltpu.VMEM((3, KP, F), F32),
            pltpu.VMEM((3, KP, F), BF),
            pltpu.VMEM((3, 2, D, F), BF),
            pltpu.VMEM((3, D, F), BF),
            pltpu.VMEM((3, D, F), BF),
            pltpu.SemaphoreType.DMA((n_links,)),
            pltpu.SemaphoreType.DMA((n_links,)),
            pltpu.SemaphoreType.DMA((6,)),
        ],
        compiler_params=pltpu.CompilerParams(
            collective_id=0, has_side_effects=True, vmem_limit_bytes=62 * 1024 * 1024
        ),
    )(inputs, curvature, w_gate, w_up, v_gate, v_up, w_down.T, v_down.T)
    return to, pg, pu, pd.T


def solution(mesh):
    ndp, nt = mesh.shape["dp"], mesh.shape["tensor"]
    return jax.shard_map(
        functools.partial(on_device, ndp // 4, nt),
        mesh=mesh,
        in_specs=(
            P(("dp", "tensor"), None),
            P(("dp", "tensor")),
            P("dp", "tensor"),
            P("dp", "tensor"),
            P("tensor", "dp"),
            P("dp", "tensor"),
            P("dp", "tensor"),
            P("tensor", "dp"),
        ),
        out_specs=(
            P(("dp", "tensor"), None),
            P("dp", "tensor"),
            P("dp", "tensor"),
            P("tensor", "dp"),
        ),
        check_vma=False,
    )
```

```python
import functools

import jax
import jax.numpy as jnp
from jax import lax
from jax.experimental import pallas as pl
from jax.experimental.pallas import tpu as pltpu
from jax.sharding import PartitionSpec as P

MESH = pl.DeviceIdType.MESH
BF = jnp.bfloat16
F32 = jnp.float32


def dot(a, b, ca, cb):
    return lax.dot_general(a, b, (((ca,), (cb,)), ((), ())), preferred_element_type=F32)


class Link:
    def __init__(self, sems, slot, src, dst, device):
        self.copy = pltpu.make_async_remote_copy(
            src_ref=src,
            dst_ref=dst,
            send_sem=sems[0].at[slot],
            recv_sem=sems[1].at[slot],
            device_id=device,
            device_id_type=MESH,
        )
        self.copy.start()

    def arrive(self):
        self.copy.wait_recv()

    def left(self):
        self.copy.wait_send()


def kernel(
    NY, NT, D, F, KP,
    x_in, curv_in, wg, wu, vg, vu, wd, vd,
    to, pg, pu, pd,
    stage, xin, X, W, Pf, Pd, rs_s, rs_r, dh_s, dh_r, H, A, G,
    Tf, Tb, trecv, wt, osend, orecv, ot, PF, PB, C1, zs, zr,
    send_sems, recv_sems, local_sems,
):
    K = 4 * D
    R = 2 * NY
    C = 2 * NT
    M = NT * R
    NX = 4 if NT % 4 == 0 else 1
    NH = NT // NX
    dp = lax.axis_index("dp")
    t = lax.axis_index("tensor")
    c = lax.rem(dp, 2)
    y = lax.rem(lax.div(dp, 2), NY)
    z = lax.div(dp, 2 * NY)

    def at(zz, yy, cc):
        return ((zz * NY + yy) * 2 + cc, t)

    core = at(z, y, 1 - c)
    zed = at(1 - z, y, c)

    def up_y(r):
        return lax.rem(y + r + NY, NY)

    def up_t(r):
        return lax.rem(t + r, NT)

    ypeers = [at(z, up_y(r), c) for r in range(1, NY)]
    tpeers = [(dp, up_t(r)) for r in range(1, NT)]
    xq, h = lax.rem(t, NX), lax.div(t, NX)

    def up_h(r):
        return lax.rem(h + r, NH) * NX + xq

    hpeers = [(dp, up_h(r)) for r in range(1, NH)]
    xpeers = [(dp, h * NX + lax.rem(xq + r, NX)) for r in range(1, NX)]

    barrier = pltpu.get_barrier_semaphore()
    peers = [core, zed] + ypeers + tpeers
    for peer in peers:
        pl.semaphore_signal(barrier, inc=1, device_id=peer, device_id_type=MESH)

    links = []
    count = [0]

    def send(src, dst, device):
        link = Link((send_sems, recv_sems), count[0], src, dst, device)
        count[0] += 1
        links.append(link)
        return link

    def rows(q):
        return pl.ds(pl.multiple_of(q * D, 16), D)

    def chunk(j, size):
        return pl.ds(pl.multiple_of(j * size, size), size)

    row = lax.broadcasted_iota(jnp.int32, (R, KP), 0)
    lane = lax.broadcasted_iota(jnp.int32, (R, KP), 1)
    raw = x_in[...].astype(F32)
    tail = lax.broadcasted_iota(jnp.int32, (2, KP - K), 0)
    tail = jnp.where(tail == 0, curv_in[0], curv_in[1])
    for j in range(NY):
        parts = [raw[:, (zz * NY + j) * 2 * D : (zz * NY + j + 1) * 2 * D] for zz in (0, 1)]
        a = jnp.concatenate(parts + [tail], axis=1)
        a = jnp.where(row == 2 * y, a[0:1], jnp.where(row == 2 * y + 1, a[1:2], 0.0))
        hi = a.astype(BF).astype(F32)
        mid = (a - hi).astype(BF).astype(F32)
        low = a - hi - mid
        stage[j] = jnp.where(lane == K + 1, mid, jnp.where(lane == K + 2, low, hi)).astype(BF)
    pl.semaphore_wait(barrier, len(peers))

    xa = [send(stage.at[up_y(r)], xin.at[r - 1], ypeers[r - 1]) for r in range(1, NY)]

    own, other = z * 2 + c, (1 - z) * 2 + c
    mats = (wg, wu, vg, vu, wd, vd)
    locals_, from_core, from_z, forwards = {}, {}, {}, {}

    def fetch(k):
        dst = W.at[k, rows(own)]
        from_z[k] = send(mats[k], dst, zed)
        from_core[k] = send(mats[k], dst, core)
        locals_[k] = pltpu.make_async_copy(mats[k], dst, local_sems.at[k])
        locals_[k].start()

    def forward(k):
        from_z[k].arrive()
        forwards[k] = send(W.at[k, rows(other)], W.at[k, rows(other)], core)

    def have(k):
        locals_[k].wait()
        from_core[k].arrive()
        forwards[k].arrive()

    fetch(0)
    fetch(1)
    if KP > K:
        for k in range(6):
            W[k, K:KP, :] = jnp.zeros((KP - K, F), BF)

    x16 = stage[y].astype(F32)
    for r in range(1, NY):
        xa[r - 1].arrive()
        x16 = x16 + xin[r - 1].astype(F32)
    curv = x16[:, K : K + 1] + x16[:, K + 1 : K + 2] + x16[:, K + 2 : K + 3]
    X[chunk(t, R)] = x16.astype(BF)

    def all_tensor(buf):
        got = [send(buf.at[chunk(t, R)], buf.at[chunk(t, R)], p) for p in hpeers]

        def second():
            block = {}
            mine = [buf.at[chunk(t, R)]] + [buf.at[chunk(up_h(r), R)] for r in range(1, NH)]
            for n, ref in enumerate(mine):
                if n:
                    got[NH - 1 - n].arrive()
                for p in xpeers:
                    block[n, len(block)] = send(ref, ref, p)
            return list(block.values())

        return second

    second = all_tensor(X)
    fetch(2)
    xg = second()
    fetch(3)
    forward(0)
    forward(1)
    for link in xg:
        link.arrive()
    x = X[...]

    def dist(d, n):
        return at(z, up_y(d * n), c)

    def reach(k, d):
        return NY // 2 - (1 if (k % 2 == 0) == (d > 0) else 0)

    def reduce_ring(k, part, sent, recv):
        got = {}

        def step(s):
            for i, d in enumerate((-1, 1)):
                n = reach(k, d)
                if s > n:
                    continue
                v = part(k, up_y(d * (n - s + 1)))
                if s > 1:
                    got[i].arrive()
                    v = v + recv[k, i, s - 2].astype(F32)
                sent[k, i, s - 1] = v.astype(BF)
                got[i] = send(sent.at[k, i, s - 1], recv.at[k, i, s - 1], dist(d, 1))

        def total():
            v = part(k, y)
            for i, d in enumerate((-1, 1)):
                if reach(k, d):
                    got[i].arrive()
                    v = v + recv[k, i, reach(k, d) - 1].astype(F32)
            return v

        return {s: functools.partial(step, s) for s in range(1, NY // 2 + 1)}, total

    def reduce_tree(k, part, sent, recv):
        got = {}

        def push(i, d, slot, v, far):
            sent[k, i, slot] = v.astype(BF)
            got[i, slot] = send(sent.at[k, i, slot], recv.at[k, i, slot], dist(d, far))

        def first():
            for i, d in enumerate((-1, 1)):
                if reach(k, d) == 4:
                    push(i, d, 0, part(k, up_y(4 * d)), 2)
                push(i, d, 1, part(k, up_y(3 * d)), 1)
            for i, d in enumerate((-1, 1)):
                push(i, d, 2, part(k, up_y(d)), 1)

        def second():
            for i, d in enumerate((-1, 1)):
                v = part(k, up_y(2 * d))
                for slot in (1, 0) if reach(k, d) == 4 else (1,):
                    got[i, slot].arrive()
                    v = v + recv[k, i, slot].astype(F32)
                push(i, d, 3, v, 2)

        def total():
            v = part(k, y)
            for slot in (2, 3):
                for i in (0, 1):
                    got[i, slot].arrive()
                    v = v + recv[k, i, slot].astype(F32)
            return v

        return {1: first, 2: second}, total

    def gather_ring(k, ref):
        got = {}

        def step(s):
            for i, d in enumerate((-1, 1)):
                if s > reach(k, d):
                    continue
                if s > 1:
                    got[i].arrive()
                block = ref(up_y(-d * (s - 1)))
                got[i] = send(block, block, dist(d, 1))

        def finish():
            for i in got:
                got[i].arrive()

        return {s: functools.partial(step, s) for s in range(1, NY // 2 + 1)}, finish

    def gather_tree(k, ref):
        got = {}

        def first():
            for far in (2, 1):
                for i, d in enumerate((-1, 1)):
                    got[i, 2 - far] = send(ref(y), ref(y), dist(d, far))

        def second():
            for i, d in enumerate((-1, 1)):
                got[i, 0].arrive()
                block = ref(up_y(-2 * d))
                if reach(k, d) == 4:
                    got[i, 3] = send(block, block, dist(d, 2))
                got[i, 2] = send(block, block, dist(d, 1))

        def finish():
            for i, slot in got:
                if slot:
                    got[i, slot].arrive()

        return {1: first, 2: second}, finish

    def in_waves(plans, late=None, between=None):
        steps = []
        for n, (waves, _) in enumerate(plans):
            steps += [(w + (late[n] if late else 0), n, f) for w, f in waves.items()]
        last = None
        for w, n, f in sorted(steps, key=lambda e: e[:2]):
            if between and last is not None and w != last and last in between:
                between[last]()
            last = w
            f()

    if NY != 8:
        reduce_tree, gather_tree = reduce_ring, gather_ring

    def part(k, j):
        return Pf[k, chunk(j, C)]

    def begin(k):
        have(k)
        Pf[k] = dot(x, W[k], 1, 0)

    plans = []
    for k in range(4):
        waves, total = reduce_ring(k, part, rs_s, rs_r)

        def opened(k=k, step=waves[1]):
            begin(k)
            step()

        waves[1] = opened
        plans.append((waves, total))

    def more():
        forward(2)
        forward(3)

    def down():
        fetch(4)
        fetch(5)

    in_waves(plans, (0, 0, 1, 1), {1: more, 2: down} if NY == 8 else {1: lambda: (more(), down())})
    gate, up, dgate, dup = [total() for _, total in plans]
    sig = jax.nn.sigmoid(gate)
    act = gate * sig
    slope = sig * (1.0 + gate * (1.0 - sig))
    up_slope = up * slope
    H[0, chunk(y, C)] = (act * up).astype(BF)
    H[1, chunk(y, C)] = (up_slope * dgate + act * dup).astype(BF)
    A[0, chunk(y, C)] = act.astype(BF)
    A[1, chunk(y, C)] = up_slope.astype(BF)
    half = C // 2

    def piece(buf, n, q):
        return lambda j: buf.at[n, pl.ds(pl.multiple_of(j * C + q * half, half), half)]

    plans = [gather_ring(q, piece(H, n, q)) for n in (0, 1) for q in (0, 1)]
    in_waves(plans)
    forward(4)
    forward(5)
    have(4)
    have(5)
    plans[0][1]()
    plans[1][1]()
    tangent = dot(H[0], W[5], 1, 1)
    plans[2][1]()
    plans[3][1]()
    tangent = tangent + dot(H[1], W[4], 1, 1)

    Tf[...] = tangent
    Tb[...] = tangent.astype(BF)
    tr = [send(Tb.at[chunk(up_t(r), R)], trecv.at[r - 1], tpeers[r - 1]) for r in range(1, NT)]
    aplans = [gather_tree(n, lambda j, n=n: A.at[n, chunk(j, C)]) for n in (0, 1)]
    aplans[0][0][1]()
    aplans[1][0][1]()
    total = Tf[chunk(t, R)]
    for r in range(1, NT):
        tr[r - 1].arrive()
        total = total + trecv[r - 1].astype(F32)
    wt[chunk(t, R)] = (curv * total).astype(BF)
    tw = [send(wt.at[chunk(t, R)], wt.at[chunk(t, R)], p) for p in tpeers]
    osend[...] = total.astype(BF)
    oa = [send(osend, orecv.at[r - 1], ypeers[r - 1]) for r in range(1, NY)]
    for w in sorted(aplans[0][0])[1:]:
        aplans[0][0][w]()
        aplans[1][0][w]()
    for link in tw:
        link.arrive()
    weighted = wt[...]

    Pd[...] = dot(weighted, W[4], 1, 0)

    def part_of(k, j):
        return Pd[pl.ds(pl.multiple_of(j * C + k * half, half), half)]

    stage1, stage2 = {}, {}

    def product(i, lhs, rhs):
        full = dot(lhs, rhs, 0, 0)
        PF[i] = full
        PB[i] = full.astype(BF)
        for n, zz in enumerate((1 - z, z)):
            stage1[i, n] = send(PB.at[i, rows(zz * 2 + 1 - c)], C1.at[i, n], core)

    def cross(i):
        stage1[i, 0].arrive()
        zs[i] = (PF[i, rows((1 - z) * 2 + c)] + C1[i, 0].astype(F32)).astype(BF)
        stage2[i] = send(zs.at[i], zr.at[i], zed)

    def settle(i, out):
        stage1[i, 1].arrive()
        mine = PF[i, rows(z * 2 + c)] + C1[i, 1].astype(F32)
        stage2[i].arrive()
        out[...] = mine + zr[i].astype(F32)

    plans = [reduce_tree(k, part_of, dh_s, dh_r) for k in (0, 1)]
    in_waves(plans, None, {1: lambda: product(2, weighted, H[0])} if NY == 8 else None)
    for k, (_, total) in enumerate(plans):
        G[pl.ds(pl.multiple_of(y * C + k * half, half), half)] = total().astype(BF)
    if NY != 8:
        product(2, weighted, H[0])
    plans = [gather_tree(k, lambda j, k=k: G.at[pl.ds(pl.multiple_of(j * C + k * half, half), half)]) for k in (0, 1)]
    in_waves(plans)
    for _, finish in aplans:
        finish()
    cross(2)

    def two_rows(v):
        v = v.astype(F32)
        return [jnp.sum(jnp.where(row == 2 * y + i, v, 0.0), axis=0, keepdims=True) for i in (0, 1)]

    for r in range(NY):
        if r:
            oa[r - 1].arrive()
        a, b = two_rows(orecv[r - 1] if r else osend[...])
        ot[up_y(-r)] = jnp.concatenate([a, b], axis=0)
    for j in range(NY):
        v = ot[j].astype(BF)
        for zz in (0, 1):
            to[:, (zz * NY + j) * 2 * D : (zz * NY + j + 1) * 2 * D] = v[:, zz * 2 * D : (zz + 1) * 2 * D]
    settle(2, pd)

    for _, finish in plans:
        finish()
    dhid = G[...].astype(F32)
    product(0, x, (dhid * A[1].astype(F32)).astype(BF))
    product(1, x, (dhid * A[0].astype(F32)).astype(BF))
    cross(0)
    cross(1)
    settle(0, pg)
    settle(1, pu)
    for link in links:
        link.left()


def hand_on(*refs):
    for i in range(4):
        refs[4 + i][...] = refs[i][...]


def on_device(NY, NT, inputs, curvature, w_gate, w_up, w_down, v_gate, v_up, v_down):
    D, F = w_gate.shape
    K = 4 * D
    KP = -(-(K + 3) // 128) * 128
    R, C = 2 * NY, 2 * NT
    M = NT * R
    steps = NY // 2
    n_links = 2 * (NY - 1) + 3 * (NT - 1) + 18 + 9 + 14 * (NY - 1)
    vmem = pl.BlockSpec(memory_space=pltpu.VMEM)
    hbm = pl.BlockSpec(memory_space=pl.ANY)
    to, pg, pu, pd = pl.pallas_call(
        functools.partial(kernel, NY, NT, D, F, KP),
        out_shape=[
            jax.ShapeDtypeStruct((2, 4 * NY * D), BF),
            jax.ShapeDtypeStruct((D, F), F32),
            jax.ShapeDtypeStruct((D, F), F32),
            jax.ShapeDtypeStruct((D, F), F32),
        ],
        in_specs=[vmem, pl.BlockSpec(memory_space=pltpu.SMEM)] + [hbm] * 6,
        out_specs=[vmem] * 4,
        scratch_shapes=[
            pltpu.VMEM((NY, R, KP), BF),
            pltpu.VMEM((NY - 1, R, KP), BF),
            pltpu.VMEM((M, KP), BF),
            pltpu.VMEM((6, KP, F), BF),
            pltpu.VMEM((4, M, F), F32),
            pltpu.VMEM((M, F), F32),
            pltpu.VMEM((4, 2, steps, C, F), BF),
            pltpu.VMEM((4, 2, steps, C, F), BF),
            pltpu.VMEM((2, 2, steps, C // 2, F), BF),
            pltpu.VMEM((2, 2, steps, C // 2, F), BF),
            pltpu.VMEM((2, M, F), BF),
            pltpu.VMEM((2, M, F), BF),
            pltpu.VMEM((M, F), BF),
            pltpu.VMEM((M, KP), F32),
            pltpu.VMEM((M, KP), BF),
            pltpu.VMEM((max(NT - 1, 1), R, KP), BF),
            pltpu.VMEM((M, KP), BF),
            pltpu.VMEM((R, KP), BF),
            pltpu.VMEM((NY - 1, R, KP), BF),
            pltpu.VMEM((NY, 2, KP), F32),
            pltpu.VMEM((3, KP, F), F32),
            pltpu.VMEM((3, KP, F), BF),
            pltpu.VMEM((3, 2, D, F), BF),
            pltpu.VMEM((3, D, F), BF),
            pltpu.VMEM((3, D, F), BF),
            pltpu.SemaphoreType.DMA((n_links,)),
            pltpu.SemaphoreType.DMA((n_links,)),
            pltpu.SemaphoreType.DMA((6,)),
        ],
        compiler_params=pltpu.CompilerParams(
            collective_id=0, has_side_effects=True, vmem_limit_bytes=62 * 1024 * 1024
        ),
    )(inputs, curvature, w_gate, w_up, v_gate, v_up, w_down.T, v_down.T)
    arrays = (to, pg, pu, pd)
    to, pg, pu, pd = pl.pallas_call(
        hand_on,
        out_shape=[jax.ShapeDtypeStruct(a.shape, a.dtype) for a in arrays],
        in_specs=[vmem] * 4,
        out_specs=[vmem] * 4,
    )(*arrays)
    return to, pg, pu, pd.T


def solution(mesh):
    ndp, nt = mesh.shape["dp"], mesh.shape["tensor"]
    return jax.shard_map(
        functools.partial(on_device, ndp // 4, nt),
        mesh=mesh,
        in_specs=(
            P(("dp", "tensor"), None),
            P(("dp", "tensor")),
            P("dp", "tensor"),
            P("dp", "tensor"),
            P("tensor", "dp"),
            P("dp", "tensor"),
            P("dp", "tensor"),
            P("tensor", "dp"),
        ),
        out_specs=(
            P(("dp", "tensor"), None),
            P("dp", "tensor"),
            P("dp", "tensor"),
            P("tensor", "dp"),
        ),
        check_vma=False,
    )
```

```python
import functools

import jax
import jax.numpy as jnp
from jax import lax
from jax.experimental import pallas as pl
from jax.experimental.pallas import tpu as pltpu
from jax.sharding import PartitionSpec as P

MESH = pl.DeviceIdType.MESH
BF = jnp.bfloat16
F32 = jnp.float32


def dot(a, b, ca, cb):
    return lax.dot_general(a, b, (((ca,), (cb,)), ((), ())), preferred_element_type=F32)


class Link:
    def __init__(self, sems, slot, src, dst, device):
        self.copy = pltpu.make_async_remote_copy(
            src_ref=src,
            dst_ref=dst,
            send_sem=sems[0].at[slot],
            recv_sem=sems[1].at[slot],
            device_id=device,
            device_id_type=MESH,
        )
        self.copy.start()

    def arrive(self):
        self.copy.wait_recv()

    def left(self):
        self.copy.wait_send()


def kernel(
    NY, NT, D, F, KP,
    x_in, curv_in, wg, wu, vg, vu, wd, vd,
    to, pg, pu, pd,
    stage, xin, X, W, Pf, Pd, rs_s, rs_r, dh_s, dh_r, H, A, G,
    Tf, Tb, trecv, wt, osend, orecv, ot, PF, PB, C1, zs, zr,
    send_sems, recv_sems, local_sems,
):
    K = 4 * D
    R = 2 * NY
    C = 2 * NT
    M = NT * R
    NX = 4 if NT % 4 == 0 else 1
    NH = NT // NX
    dp = lax.axis_index("dp")
    t = lax.axis_index("tensor")
    c = lax.rem(dp, 2)
    y = lax.rem(lax.div(dp, 2), NY)
    z = lax.div(dp, 2 * NY)

    def at(zz, yy, cc):
        return ((zz * NY + yy) * 2 + cc, t)

    core = at(z, y, 1 - c)
    zed = at(1 - z, y, c)

    def up_y(r):
        return lax.rem(y + r + NY, NY)

    def up_t(r):
        return lax.rem(t + r, NT)

    ypeers = [at(z, up_y(r), c) for r in range(1, NY)]
    tpeers = [(dp, up_t(r)) for r in range(1, NT)]
    xq, h = lax.rem(t, NX), lax.div(t, NX)

    def up_h(r):
        return lax.rem(h + r, NH) * NX + xq

    hpeers = [(dp, up_h(r)) for r in range(1, NH)]
    xpeers = [(dp, h * NX + lax.rem(xq + r, NX)) for r in range(1, NX)]

    barrier = pltpu.get_barrier_semaphore()
    peers = [core, zed] + ypeers + tpeers
    for peer in peers:
        pl.semaphore_signal(barrier, inc=1, device_id=peer, device_id_type=MESH)

    links = []
    count = [0]

    def send(src, dst, device):
        link = Link((send_sems, recv_sems), count[0], src, dst, device)
        count[0] += 1
        links.append(link)
        return link

    def rows(q):
        return pl.ds(pl.multiple_of(q * D, 16), D)

    def chunk(j, size):
        return pl.ds(pl.multiple_of(j * size, size), size)

    row = lax.broadcasted_iota(jnp.int32, (R, KP), 0)
    lane = lax.broadcasted_iota(jnp.int32, (R, KP), 1)
    raw = x_in[...].astype(F32)
    tail = lax.broadcasted_iota(jnp.int32, (2, KP - K), 0)
    tail = jnp.where(tail == 0, curv_in[0], curv_in[1])
    for j in range(NY):
        parts = [raw[:, (zz * NY + j) * 2 * D : (zz * NY + j + 1) * 2 * D] for zz in (0, 1)]
        a = jnp.concatenate(parts + [tail], axis=1)
        a = jnp.where(row == 2 * y, a[0:1], jnp.where(row == 2 * y + 1, a[1:2], 0.0))
        hi = a.astype(BF).astype(F32)
        mid = (a - hi).astype(BF).astype(F32)
        low = a - hi - mid
        stage[j] = jnp.where(lane == K + 1, mid, jnp.where(lane == K + 2, low, hi)).astype(BF)
    pl.semaphore_wait(barrier, len(peers))

    y_order = sorted(range(1, NY), key=lambda r: abs(r - NY // 2))
    xa = {r - 1: send(stage.at[up_y(r)], xin.at[r - 1], ypeers[r - 1]) for r in y_order}

    own, other = z * 2 + c, (1 - z) * 2 + c
    mats = (wg, wu, vg, vu, wd, vd)
    locals_, from_core, from_z, forwards = {}, {}, {}, {}

    def fetch(k):
        dst = W.at[k, rows(own)]
        from_z[k] = send(mats[k], dst, zed)
        from_core[k] = send(mats[k], dst, core)
        locals_[k] = pltpu.make_async_copy(mats[k], dst, local_sems.at[k])
        locals_[k].start()

    def forward(k):
        from_z[k].arrive()
        forwards[k] = send(W.at[k, rows(other)], W.at[k, rows(other)], core)

    def have(k):
        locals_[k].wait()
        from_core[k].arrive()
        forwards[k].arrive()

    fetch(0)
    if KP > K:
        for k in range(6):
            W[k, K:KP, :] = jnp.zeros((KP - K, F), BF)

    x16 = stage[y].astype(F32)
    for r in reversed(y_order):
        xa[r - 1].arrive()
        x16 = x16 + xin[r - 1].astype(F32)
    curv = x16[:, K : K + 1] + x16[:, K + 1 : K + 2] + x16[:, K + 2 : K + 3]
    X[chunk(t, R)] = x16.astype(BF)

    def all_tensor(buf):
        h_order = sorted(range(1, NH), key=lambda r: abs(r - NH // 2))
        got = {r: send(buf.at[chunk(t, R)], buf.at[chunk(t, R)], hpeers[r - 1]) for r in h_order}

        def second():
            block = {}
            mine = [buf.at[chunk(t, R)]] + [buf.at[chunk(up_h(r), R)] for r in range(1, NH)]
            for n in [0] + h_order[::-1]:
                ref = mine[n]
                if n:
                    got[NH - n].arrive()
                for p in xpeers:
                    block[n, len(block)] = send(ref, ref, p)
            return list(block.values())

        return second

    second = all_tensor(X)
    fetch(1)
    xg = second()
    fetch(2)
    fetch(3)
    forward(0)
    forward(1)
    for link in xg:
        link.arrive()
    x = X[...]

    def dist(d, n):
        return at(z, up_y(d * n), c)

    def reach(k, d):
        return NY // 2 - (1 if (k % 2 == 0) == (d > 0) else 0)

    def reduce_ring(k, part, sent, recv):
        got = {}

        def step(s):
            for i, d in enumerate((-1, 1)):
                n = reach(k, d)
                if s > n:
                    continue
                v = part(k, up_y(d * (n - s + 1)))
                if s > 1:
                    got[i].arrive()
                    v = v + recv[k, i, s - 2].astype(F32)
                sent[k, i, s - 1] = v.astype(BF)
                got[i] = send(sent.at[k, i, s - 1], recv.at[k, i, s - 1], dist(d, 1))

        def total():
            v = part(k, y)
            for i, d in enumerate((-1, 1)):
                if reach(k, d):
                    got[i].arrive()
                    v = v + recv[k, i, reach(k, d) - 1].astype(F32)
            return v

        return {s: functools.partial(step, s) for s in range(1, NY // 2 + 1)}, total

    def reduce_tree(k, part, sent, recv):
        got = {}

        def push(i, d, slot, v, far):
            sent[k, i, slot] = v.astype(BF)
            got[i, slot] = send(sent.at[k, i, slot], recv.at[k, i, slot], dist(d, far))

        def first():
            for i, d in enumerate((-1, 1)):
                if reach(k, d) == 4:
                    push(i, d, 0, part(k, up_y(4 * d)), 2)
                push(i, d, 1, part(k, up_y(3 * d)), 1)
            for i, d in enumerate((-1, 1)):
                push(i, d, 2, part(k, up_y(d)), 1)

        def second():
            for i, d in enumerate((-1, 1)):
                v = part(k, up_y(2 * d))
                for slot in (1, 0) if reach(k, d) == 4 else (1,):
                    got[i, slot].arrive()
                    v = v + recv[k, i, slot].astype(F32)
                push(i, d, 3, v, 2)

        def total():
            v = part(k, y)
            for slot in (2, 3):
                for i in (0, 1):
                    got[i, slot].arrive()
                    v = v + recv[k, i, slot].astype(F32)
            return v

        return {1: first, 2: second}, total

    def gather_ring(k, ref):
        got = {}

        def step(s):
            for i, d in enumerate((-1, 1)):
                if s > reach(k, d):
                    continue
                if s > 1:
                    got[i].arrive()
                block = ref(up_y(-d * (s - 1)))
                got[i] = send(block, block, dist(d, 1))

        def finish():
            for i in got:
                got[i].arrive()

        return {s: functools.partial(step, s) for s in range(1, NY // 2 + 1)}, finish

    def gather_tree(k, ref):
        got = {}

        def first():
            for far in (2, 1):
                for i, d in enumerate((-1, 1)):
                    got[i, 2 - far] = send(ref(y), ref(y), dist(d, far))

        def second():
            for i, d in enumerate((-1, 1)):
                got[i, 0].arrive()
                block = ref(up_y(-2 * d))
                if reach(k, d) == 4:
                    got[i, 3] = send(block, block, dist(d, 2))
                got[i, 2] = send(block, block, dist(d, 1))

        def finish():
            for i, slot in got:
                if slot:
                    got[i, slot].arrive()

        return {1: first, 2: second}, finish

    def in_waves(plans, late=None, between=None):
        steps = []
        for n, (waves, _) in enumerate(plans):
            steps += [(w + (late[n] if late else 0), n, f) for w, f in waves.items()]
        last = None
        for w, n, f in sorted(steps, key=lambda e: e[:2]):
            if between and last is not None and w != last and last in between:
                between[last]()
            last = w
            f()

    if NY != 8:
        reduce_tree, gather_tree = reduce_ring, gather_ring

    def part(k, j):
        return Pf[k, chunk(j, C)]

    def begin(k):
        if k >= 2:
            forward(k)
        have(k)
        Pf[k] = dot(x, W[k], 1, 0)

    plans = []
    for k in range(4):
        waves, total = reduce_ring(k, part, rs_s, rs_r)

        def opened(k=k, step=waves[1]):
            begin(k)
            step()

        waves[1] = opened
        plans.append((waves, total))

    def down():
        fetch(4)
        fetch(5)

    in_waves(plans, None, {1: down} if NY > 2 else None)
    if NY == 2:
        down()
    half = C // 2

    def piece(buf, n, q):
        return lambda j: buf.at[n, pl.ds(pl.multiple_of(j * C + q * half, half), half)]

    def steps_of(pair, w):
        for waves, _ in pair:
            if w in waves:
                waves[w]()

    gate, up = plans[0][1](), plans[1][1]()
    sig = jax.nn.sigmoid(gate)
    act = gate * sig
    slope = sig * (1.0 + gate * (1.0 - sig))
    up_slope = up * slope
    H[0, chunk(y, C)] = (act * up).astype(BF)
    hid = [gather_tree(q, piece(H, 0, q)) for q in (0, 1)]
    steps_of(hid, 1)
    A[0, chunk(y, C)] = act.astype(BF)
    A[1, chunk(y, C)] = up_slope.astype(BF)
    dgate, dup = plans[2][1](), plans[3][1]()
    H[1, chunk(y, C)] = (up_slope * dgate + act * dup).astype(BF)
    thid = [gather_tree(q, piece(H, 1, q)) for q in (0, 1)]
    steps_of(thid, 1)
    for w in range(2, NY // 2 + 1):
        steps_of(hid, w)
        steps_of(thid, w)
    plans = hid + thid
    forward(4)
    forward(5)
    have(4)
    have(5)
    plans[0][1]()
    plans[1][1]()
    tangent = dot(H[0], W[5], 1, 1)
    plans[2][1]()
    plans[3][1]()
    tangent = tangent + dot(H[1], W[4], 1, 1)

    Tf[...] = tangent
    Tb[...] = tangent.astype(BF)
    far_first = sorted(range(1, NT), key=lambda r: abs(r - NT // 2))
    tr = {r - 1: send(Tb.at[chunk(up_t(r), R)], trecv.at[r - 1], tpeers[r - 1]) for r in far_first}
    aplans = [gather_tree(n, lambda j, n=n: A.at[n, chunk(j, C)]) for n in (0, 1)]
    aplans[0][0][1]()
    aplans[1][0][1]()
    total = Tf[chunk(t, R)]
    for r in range(1, NT):
        tr[r - 1].arrive()
        total = total + trecv[r - 1].astype(F32)
    wt[chunk(t, R)] = (curv * total).astype(BF)
    tw = [send(wt.at[chunk(t, R)], wt.at[chunk(t, R)], tpeers[r - 1]) for r in far_first]
    osend[...] = total.astype(BF)
    oa = [send(osend, orecv.at[r - 1], ypeers[r - 1]) for r in range(1, NY)]
    for w in sorted(aplans[0][0])[1:]:
        aplans[0][0][w]()
        aplans[1][0][w]()
    for link in tw:
        link.arrive()
    weighted = wt[...]

    Pd[...] = dot(weighted, W[4], 1, 0)

    def part_of(k, j):
        return Pd[pl.ds(pl.multiple_of(j * C + k * half, half), half)]

    stage1, stage2 = {}, {}

    def product(i, lhs, rhs):
        full = dot(lhs, rhs, 0, 0)
        PF[i] = full
        PB[i] = full.astype(BF)
        for n, zz in enumerate((1 - z, z)):
            stage1[i, n] = send(PB.at[i, rows(zz * 2 + 1 - c)], C1.at[i, n], core)

    def cross(i):
        stage1[i, 0].arrive()
        zs[i] = (PF[i, rows((1 - z) * 2 + c)] + C1[i, 0].astype(F32)).astype(BF)
        stage2[i] = send(zs.at[i], zr.at[i], zed)

    def settle(i, out):
        stage1[i, 1].arrive()
        mine = PF[i, rows(z * 2 + c)] + C1[i, 1].astype(F32)
        stage2[i].arrive()
        out[...] = mine + zr[i].astype(F32)

    plans = [reduce_tree(k, part_of, dh_s, dh_r) for k in (0, 1)]
    in_waves(plans, None, {1: lambda: product(2, weighted, H[0])} if NY == 8 else None)
    for k, (_, total) in enumerate(plans):
        G[pl.ds(pl.multiple_of(y * C + k * half, half), half)] = total().astype(BF)
    if NY != 8:
        product(2, weighted, H[0])
    plans = [gather_tree(k, lambda j, k=k: G.at[pl.ds(pl.multiple_of(j * C + k * half, half), half)]) for k in (0, 1)]
    in_waves(plans)
    for _, finish in aplans:
        finish()
    cross(2)

    def two_rows(v):
        v = v.astype(F32)
        return [jnp.sum(jnp.where(row == 2 * y + i, v, 0.0), axis=0, keepdims=True) for i in (0, 1)]

    for r in range(NY):
        if r:
            oa[r - 1].arrive()
        a, b = two_rows(orecv[r - 1] if r else osend[...])
        ot[up_y(-r)] = jnp.concatenate([a, b], axis=0)
    for j in range(NY):
        v = ot[j].astype(BF)
        for zz in (0, 1):
            to[:, (zz * NY + j) * 2 * D : (zz * NY + j + 1) * 2 * D] = v[:, zz * 2 * D : (zz + 1) * 2 * D]
    settle(2, pd)

    for _, finish in plans:
        finish()
    dhid = G[...].astype(F32)
    product(0, x, (dhid * A[1].astype(F32)).astype(BF))
    bup = (dhid * A[0].astype(F32)).astype(BF)
    cross(0)
    product(1, x, bup)
    cross(1)
    settle(0, pg)
    settle(1, pu)
    for link in links:
        link.left()


def hand_on(*refs):
    for i in range(4):
        refs[4 + i][...] = refs[i][...]


def on_device(NY, NT, inputs, curvature, w_gate, w_up, w_down, v_gate, v_up, v_down):
    D, F = w_gate.shape
    K = 4 * D
    KP = -(-(K + 3) // 128) * 128
    R, C = 2 * NY, 2 * NT
    M = NT * R
    steps = NY // 2
    n_links = 2 * (NY - 1) + 3 * (NT - 1) + 18 + 9 + 14 * (NY - 1)
    vmem = pl.BlockSpec(memory_space=pltpu.VMEM)
    hbm = pl.BlockSpec(memory_space=pl.ANY)
    to, pg, pu, pd = pl.pallas_call(
        functools.partial(kernel, NY, NT, D, F, KP),
        out_shape=[
            jax.ShapeDtypeStruct((2, 4 * NY * D), BF),
            jax.ShapeDtypeStruct((D, F), F32),
            jax.ShapeDtypeStruct((D, F), F32),
            jax.ShapeDtypeStruct((D, F), F32),
        ],
        in_specs=[vmem, pl.BlockSpec(memory_space=pltpu.SMEM)] + [hbm] * 6,
        out_specs=[vmem] * 4,
        scratch_shapes=[
            pltpu.VMEM((NY, R, KP), BF),
            pltpu.VMEM((NY - 1, R, KP), BF),
            pltpu.VMEM((M, KP), BF),
            pltpu.VMEM((6, KP, F), BF),
            pltpu.VMEM((4, M, F), F32),
            pltpu.VMEM((M, F), F32),
            pltpu.VMEM((4, 2, steps, C, F), BF),
            pltpu.VMEM((4, 2, steps, C, F), BF),
            pltpu.VMEM((2, 2, steps, C // 2, F), BF),
            pltpu.VMEM((2, 2, steps, C // 2, F), BF),
            pltpu.VMEM((2, M, F), BF),
            pltpu.VMEM((2, M, F), BF),
            pltpu.VMEM((M, F), BF),
            pltpu.VMEM((M, KP), F32),
            pltpu.VMEM((M, KP), BF),
            pltpu.VMEM((max(NT - 1, 1), R, KP), BF),
            pltpu.VMEM((M, KP), BF),
            pltpu.VMEM((R, KP), BF),
            pltpu.VMEM((NY - 1, R, KP), BF),
            pltpu.VMEM((NY, 2, KP), F32),
            pltpu.VMEM((3, KP, F), F32),
            pltpu.VMEM((3, KP, F), BF),
            pltpu.VMEM((3, 2, D, F), BF),
            pltpu.VMEM((3, D, F), BF),
            pltpu.VMEM((3, D, F), BF),
            pltpu.SemaphoreType.DMA((n_links,)),
            pltpu.SemaphoreType.DMA((n_links,)),
            pltpu.SemaphoreType.DMA((6,)),
        ],
        compiler_params=pltpu.CompilerParams(
            collective_id=0, has_side_effects=True, vmem_limit_bytes=62 * 1024 * 1024
        ),
    )(inputs, curvature, w_gate, w_up, v_gate, v_up, w_down.T, v_down.T)
    arrays = (to, pg, pu, pd)
    to, pg, pu, pd = pl.pallas_call(
        hand_on,
        out_shape=[jax.ShapeDtypeStruct(a.shape, a.dtype) for a in arrays],
        in_specs=[vmem] * 4,
        out_specs=[vmem] * 4,
    )(*arrays)
    return to, pg, pu, pd.T


def solution(mesh):
    ndp, nt = mesh.shape["dp"], mesh.shape["tensor"]
    return jax.shard_map(
        functools.partial(on_device, ndp // 4, nt),
        mesh=mesh,
        in_specs=(
            P(("dp", "tensor"), None),
            P(("dp", "tensor")),
            P("dp", "tensor"),
            P("dp", "tensor"),
            P("tensor", "dp"),
            P("dp", "tensor"),
            P("dp", "tensor"),
            P("tensor", "dp"),
        ),
        out_specs=(
            P(("dp", "tensor"), None),
            P("dp", "tensor"),
            P("dp", "tensor"),
            P("tensor", "dp"),
        ),
        check_vma=False,
    )
```

```python
import functools

import jax
import jax.numpy as jnp
from jax import lax
from jax.experimental import pallas as pl
from jax.experimental.pallas import tpu as pltpu
from jax.sharding import PartitionSpec as P

MESH = pl.DeviceIdType.MESH
BF = jnp.bfloat16
F32 = jnp.float32


def dot(a, b, ca, cb):
    return lax.dot_general(a, b, (((ca,), (cb,)), ((), ())), preferred_element_type=F32)


def first_piece(F):
    return (F // 2 + 127) // 128 * 128 if F > 256 else F // 2


class Link:
    def __init__(self, sems, slot, src, dst, device):
        self.copy = pltpu.make_async_remote_copy(
            src_ref=src,
            dst_ref=dst,
            send_sem=sems[0].at[slot],
            recv_sem=sems[1].at[slot],
            device_id=device,
            device_id_type=MESH,
        )
        self.copy.start()

    def arrive(self):
        self.copy.wait_recv()

    def left(self):
        self.copy.wait_send()


def kernel(
    NY, NT, D, F, KP,
    x_in, curv_in, wg, wu, vg, vu, wd, vd,
    to, pg, pu, pd,
    stage, xin, X, W, Pf, Pd, rs_s, rs_r, H, A,
    Tf, Tb, trecv, wt, osend, orecv, ot, PF,
    dh_sa, dh_ra, Ga, PBa, C1a, zsa, zra,
    dh_sb, dh_rb, Gb, PBb, C1b, zsb, zrb,
    send_sems, recv_sems, local_sems,
):
    K = 4 * D
    R = 2 * NY
    C = 2 * NT
    M = NT * R
    NX = 4 if NT % 4 == 0 else 1
    NH = NT // NX
    dp = lax.axis_index("dp")
    t = lax.axis_index("tensor")
    c = lax.rem(dp, 2)
    y = lax.rem(lax.div(dp, 2), NY)
    z = lax.div(dp, 2 * NY)

    def at(zz, yy, cc):
        return ((zz * NY + yy) * 2 + cc, t)

    core = at(z, y, 1 - c)
    zed = at(1 - z, y, c)

    def up_y(r):
        return lax.rem(y + r + NY, NY)

    def up_t(r):
        return lax.rem(t + r, NT)

    ypeers = [at(z, up_y(r), c) for r in range(1, NY)]
    tpeers = [(dp, up_t(r)) for r in range(1, NT)]
    xq, h = lax.rem(t, NX), lax.div(t, NX)

    def up_h(r):
        return lax.rem(h + r, NH) * NX + xq

    hpeers = [(dp, up_h(r)) for r in range(1, NH)]
    xpeers = [(dp, h * NX + lax.rem(xq + r, NX)) for r in range(1, NX)]

    barrier = pltpu.get_barrier_semaphore()
    peers = [core, zed] + ypeers + tpeers
    for peer in peers:
        pl.semaphore_signal(barrier, inc=1, device_id=peer, device_id_type=MESH)

    links = []
    count = [0]

    def send(src, dst, device):
        link = Link((send_sems, recv_sems), count[0], src, dst, device)
        count[0] += 1
        links.append(link)
        return link

    def rows(q):
        return pl.ds(pl.multiple_of(q * D, 16), D)

    def chunk(j, size):
        return pl.ds(pl.multiple_of(j * size, size), size)

    row = lax.broadcasted_iota(jnp.int32, (R, KP), 0)
    lane = lax.broadcasted_iota(jnp.int32, (R, KP), 1)
    raw = x_in[...].astype(F32)
    tail = lax.broadcasted_iota(jnp.int32, (2, KP - K), 0)
    tail = jnp.where(tail == 0, curv_in[0], curv_in[1])
    for j in range(NY):
        parts = [raw[:, (zz * NY + j) * 2 * D : (zz * NY + j + 1) * 2 * D] for zz in (0, 1)]
        a = jnp.concatenate(parts + [tail], axis=1)
        a = jnp.where(row == 2 * y, a[0:1], jnp.where(row == 2 * y + 1, a[1:2], 0.0))
        hi = a.astype(BF).astype(F32)
        mid = (a - hi).astype(BF).astype(F32)
        low = a - hi - mid
        stage[j] = jnp.where(lane == K + 1, mid, jnp.where(lane == K + 2, low, hi)).astype(BF)
    pl.semaphore_wait(barrier, len(peers))

    y_order = sorted(range(1, NY), key=lambda r: abs(r - NY // 2))
    xa = {r - 1: send(stage.at[up_y(r)], xin.at[r - 1], ypeers[r - 1]) for r in y_order}

    own, other = z * 2 + c, (1 - z) * 2 + c
    mats = (wg, wu, vg, vu, wd, vd)
    locals_, from_core, from_z, forwards = {}, {}, {}, {}

    def fetch(k):
        dst = W.at[k, rows(own)]
        from_z[k] = send(mats[k], dst, zed)
        from_core[k] = send(mats[k], dst, core)
        locals_[k] = pltpu.make_async_copy(mats[k], dst, local_sems.at[k])
        locals_[k].start()

    def forward(k):
        from_z[k].arrive()
        forwards[k] = send(W.at[k, rows(other)], W.at[k, rows(other)], core)

    def have(k):
        locals_[k].wait()
        from_core[k].arrive()
        forwards[k].arrive()

    fetch(0)
    if KP > K:
        for k in range(6):
            W[k, K:KP, :] = jnp.zeros((KP - K, F), BF)

    x16 = stage[y].astype(F32)
    for r in reversed(y_order):
        xa[r - 1].arrive()
        x16 = x16 + xin[r - 1].astype(F32)
    curv = x16[:, K : K + 1] + x16[:, K + 1 : K + 2] + x16[:, K + 2 : K + 3]
    X[chunk(t, R)] = x16.astype(BF)

    def all_tensor(buf):
        h_order = sorted(range(1, NH), key=lambda r: abs(r - NH // 2))
        got = {r: send(buf.at[chunk(t, R)], buf.at[chunk(t, R)], hpeers[r - 1]) for r in h_order}

        def second():
            block = {}
            mine = [buf.at[chunk(t, R)]] + [buf.at[chunk(up_h(r), R)] for r in range(1, NH)]
            for n in [0] + h_order[::-1]:
                ref = mine[n]
                if n:
                    got[NH - n].arrive()
                for p in xpeers:
                    block[n, len(block)] = send(ref, ref, p)
            return list(block.values())

        return second

    second = all_tensor(X)
    fetch(1)
    xg = second()
    fetch(2)
    fetch(3)
    forward(0)
    forward(1)
    for link in xg:
        link.arrive()
    x = X[...]

    def dist(d, n):
        return at(z, up_y(d * n), c)

    def reach(k, d):
        return NY // 2 - (1 if (k % 2 == 0) == (d > 0) else 0)

    def reduce_ring(k, part, sent, recv, b=None):
        got = {}
        b = k if b is None else b

        def step(s):
            for i, d in enumerate((-1, 1)):
                n = reach(k, d)
                if s > n:
                    continue
                v = part(k, up_y(d * (n - s + 1)))
                if s > 1:
                    got[i].arrive()
                    v = v + recv[b, i, s - 2].astype(F32)
                sent[b, i, s - 1] = v.astype(BF)
                got[i] = send(sent.at[b, i, s - 1], recv.at[b, i, s - 1], dist(d, 1))

        def total():
            v = part(k, y)
            for i, d in enumerate((-1, 1)):
                if reach(k, d):
                    got[i].arrive()
                    v = v + recv[b, i, reach(k, d) - 1].astype(F32)
            return v

        return {s: functools.partial(step, s) for s in range(1, NY // 2 + 1)}, total

    def reduce_tree(k, part, sent, recv, b=None):
        got = {}
        b = k if b is None else b

        def push(i, d, slot, v, far):
            sent[b, i, slot] = v.astype(BF)
            got[i, slot] = send(sent.at[b, i, slot], recv.at[b, i, slot], dist(d, far))

        def first():
            for i, d in enumerate((-1, 1)):
                if reach(k, d) == 4:
                    push(i, d, 0, part(k, up_y(4 * d)), 2)
                push(i, d, 1, part(k, up_y(3 * d)), 1)
            for i, d in enumerate((-1, 1)):
                push(i, d, 2, part(k, up_y(d)), 1)

        def second():
            for i, d in enumerate((-1, 1)):
                v = part(k, up_y(2 * d))
                for slot in (1, 0) if reach(k, d) == 4 else (1,):
                    got[i, slot].arrive()
                    v = v + recv[b, i, slot].astype(F32)
                push(i, d, 3, v, 2)

        def total():
            v = part(k, y)
            for slot in (2, 3):
                for i in (0, 1):
                    got[i, slot].arrive()
                    v = v + recv[b, i, slot].astype(F32)
            return v

        return {1: first, 2: second}, total

    def gather_ring(k, ref):
        got = {}

        def step(s):
            for i, d in enumerate((-1, 1)):
                if s > reach(k, d):
                    continue
                if s > 1:
                    got[i].arrive()
                block = ref(up_y(-d * (s - 1)))
                got[i] = send(block, block, dist(d, 1))

        def finish():
            for i in got:
                got[i].arrive()

        return {s: functools.partial(step, s) for s in range(1, NY // 2 + 1)}, finish

    def gather_tree(k, ref):
        got = {}

        def first():
            for far in (2, 1):
                for i, d in enumerate((-1, 1)):
                    got[i, 2 - far] = send(ref(y), ref(y), dist(d, far))

        def second():
            for i, d in enumerate((-1, 1)):
                got[i, 0].arrive()
                block = ref(up_y(-2 * d))
                if reach(k, d) == 4:
                    got[i, 3] = send(block, block, dist(d, 2))
                got[i, 2] = send(block, block, dist(d, 1))

        def finish():
            for i, slot in got:
                if slot:
                    got[i, slot].arrive()

        return {1: first, 2: second}, finish

    def in_waves(plans, late=None, between=None):
        steps = []
        for n, (waves, _) in enumerate(plans):
            steps += [(w + (late[n] if late else 0), n, f) for w, f in waves.items()]
        last = None
        for w, n, f in sorted(steps, key=lambda e: e[:2]):
            if between and last is not None and w != last and last in between:
                between[last]()
            last = w
            f()

    if NY != 8:
        reduce_tree, gather_tree = reduce_ring, gather_ring

    def part(k, j):
        return Pf[k, chunk(j, C)]

    def begin(k):
        if k >= 2:
            forward(k)
        have(k)
        Pf[k] = dot(x, W[k], 1, 0)

    plans = []
    for k in range(4):
        waves, total = reduce_ring(k, part, rs_s, rs_r)

        def opened(k=k, step=waves[1]):
            begin(k)
            step()

        waves[1] = opened
        plans.append((waves, total))

    def down():
        fetch(4)
        fetch(5)

    in_waves(plans, None, {1: down} if NY > 2 else None)
    if NY == 2:
        down()
    half = C // 2

    def piece(buf, n, q):
        return lambda j: buf.at[n, pl.ds(pl.multiple_of(j * C + q * half, half), half)]

    def steps_of(pair, w):
        for waves, _ in pair:
            if w in waves:
                waves[w]()

    gate, up = plans[0][1](), plans[1][1]()
    sig = jax.nn.sigmoid(gate)
    act = gate * sig
    slope = sig * (1.0 + gate * (1.0 - sig))
    up_slope = up * slope
    H[0, chunk(y, C)] = (act * up).astype(BF)
    hid = [gather_tree(q, piece(H, 0, q)) for q in (0, 1)]
    steps_of(hid, 1)
    A[0, chunk(y, C)] = act.astype(BF)
    A[1, chunk(y, C)] = up_slope.astype(BF)
    dgate, dup = plans[2][1](), plans[3][1]()
    H[1, chunk(y, C)] = (up_slope * dgate + act * dup).astype(BF)
    thid = [gather_tree(q, piece(H, 1, q)) for q in (0, 1)]
    steps_of(thid, 1)
    for w in range(2, NY // 2 + 1):
        steps_of(hid, w)
        steps_of(thid, w)
    plans = hid + thid
    forward(4)
    forward(5)
    have(4)
    have(5)
    plans[0][1]()
    plans[1][1]()
    tangent = dot(H[0], W[5], 1, 1)
    plans[2][1]()
    plans[3][1]()
    tangent = tangent + dot(H[1], W[4], 1, 1)

    Tf[...] = tangent
    Tb[...] = tangent.astype(BF)
    far_first = sorted(range(1, NT), key=lambda r: abs(r - NT // 2))
    tr = {r - 1: send(Tb.at[chunk(up_t(r), R)], trecv.at[r - 1], tpeers[r - 1]) for r in far_first}
    aplans = [gather_tree(n, lambda j, n=n: A.at[n, chunk(j, C)]) for n in (0, 1)]
    aplans[0][0][1]()
    aplans[1][0][1]()
    total = Tf[chunk(t, R)]
    for r in range(1, NT):
        tr[r - 1].arrive()
        total = total + trecv[r - 1].astype(F32)
    wt[chunk(t, R)] = (curv * total).astype(BF)
    tw = [send(wt.at[chunk(t, R)], wt.at[chunk(t, R)], tpeers[r - 1]) for r in far_first]
    osend[...] = total.astype(BF)
    oa = [send(osend, orecv.at[r - 1], ypeers[r - 1]) for r in range(1, NY)]
    for w in sorted(aplans[0][0])[1:]:
        aplans[0][0][w]()
        aplans[1][0][w]()
    for link in tw:
        link.arrive()
    weighted = wt[...]

    Pd[...] = dot(weighted, W[4], 1, 0)

    FA = first_piece(F)
    lanes = (slice(0, FA), slice(FA, F))
    dh_s, dh_r, G = (dh_sa, dh_sb), (dh_ra, dh_rb), (Ga, Gb)
    PB, C1, zs, zr = (PBa, PBb), (C1a, C1b), (zsa, zsb), (zra, zrb)

    stage1, stage2 = {}, {}

    def product(i, q, lhs, rhs):
        full = dot(lhs, rhs, 0, 0)
        PF[i, :, lanes[q]] = full
        PB[q][i] = full.astype(BF)
        for n, zz in enumerate((1 - z, z)):
            stage1[i, q, n] = send(PB[q].at[i, rows(zz * 2 + 1 - c)], C1[q].at[i, n], core)

    def cross(i, q):
        stage1[i, q, 0].arrive()
        zs[q][i] = (PF[i, rows((1 - z) * 2 + c), lanes[q]] + C1[q][i, 0].astype(F32)).astype(BF)
        stage2[i, q] = send(zs[q].at[i], zr[q].at[i], zed)

    def settle(i, q, out):
        stage1[i, q, 1].arrive()
        mine = PF[i, rows(z * 2 + c), lanes[q]] + C1[q][i, 1].astype(F32)
        stage2[i, q].arrive()
        out[:, lanes[q]] = mine + zr[q][i].astype(F32)

    def part_of(k, j):
        return Pd[chunk(j, C), lanes[k]]

    sums = [reduce_tree(k, part_of, dh_s[k], dh_r[k], 0) for k in (0, 1)]
    steps_of(sums, 1)
    for q in (0, 1):
        product(2, q, weighted, H[0, :, lanes[q]])
    for w in range(2, NY // 2 + 1):
        steps_of(sums, w)
    back = []
    for k in (0, 1):
        G[k][chunk(y, C)] = sums[k][1]().astype(BF)
        back.append(gather_tree(k, lambda j, k=k: G[k].at[chunk(j, C)]))
        steps_of(back[k:], 1)
    for q in (0, 1):
        cross(2, q)
    for _, finish in aplans:
        finish()

    def two_rows(v):
        v = v.astype(F32)
        return [jnp.sum(jnp.where(row == 2 * y + i, v, 0.0), axis=0, keepdims=True) for i in (0, 1)]

    for r in range(NY):
        if r:
            oa[r - 1].arrive()
        a, b = two_rows(orecv[r - 1] if r else osend[...])
        ot[up_y(-r)] = jnp.concatenate([a, b], axis=0)
    for w in range(2, NY // 2 + 1):
        steps_of(back, w)
    for j in range(NY):
        v = ot[j].astype(BF)
        for zz in (0, 1):
            to[:, (zz * NY + j) * 2 * D : (zz * NY + j + 1) * 2 * D] = v[:, zz * 2 * D : (zz + 1) * 2 * D]

    for q in (0, 1):
        back[q][1]()
        dhid = G[q][...].astype(F32)
        product(0, q, x, (dhid * A[1, :, lanes[q]].astype(F32)).astype(BF))
        bup = (dhid * A[0, :, lanes[q]].astype(F32)).astype(BF)
        cross(0, q)
        product(1, q, x, bup)
        cross(1, q)
    for q in (0, 1):
        settle(2, q, pd)
        settle(0, q, pg)
        settle(1, q, pu)
    for link in links:
        link.left()


def hand_on(*refs):
    for i in range(4):
        refs[4 + i][...] = refs[i][...]


def on_device(NY, NT, inputs, curvature, w_gate, w_up, w_down, v_gate, v_up, v_down):
    D, F = w_gate.shape
    K = 4 * D
    KP = -(-(K + 3) // 128) * 128
    R, C = 2 * NY, 2 * NT
    M = NT * R
    steps = NY // 2
    FA = first_piece(F)

    def piece(n):
        return [
            pltpu.VMEM((1, 2, steps, C, n), BF),
            pltpu.VMEM((1, 2, steps, C, n), BF),
            pltpu.VMEM((M, n), BF),
            pltpu.VMEM((3, KP, n), BF),
            pltpu.VMEM((3, 2, D, n), BF),
            pltpu.VMEM((3, D, n), BF),
            pltpu.VMEM((3, D, n), BF),
        ]

    n_links = 2 * (NY - 1) + 3 * (NT - 1) + 18 + 18 + 14 * (NY - 1)
    vmem = pl.BlockSpec(memory_space=pltpu.VMEM)
    hbm = pl.BlockSpec(memory_space=pl.ANY)
    to, pg, pu, pd = pl.pallas_call(
        functools.partial(kernel, NY, NT, D, F, KP),
        out_shape=[
            jax.ShapeDtypeStruct((2, 4 * NY * D), BF),
            jax.ShapeDtypeStruct((D, F), F32),
            jax.ShapeDtypeStruct((D, F), F32),
            jax.ShapeDtypeStruct((D, F), F32),
        ],
        in_specs=[vmem, pl.BlockSpec(memory_space=pltpu.SMEM)] + [hbm] * 6,
        out_specs=[vmem] * 4,
        scratch_shapes=[
            pltpu.VMEM((NY, R, KP), BF),
            pltpu.VMEM((NY - 1, R, KP), BF),
            pltpu.VMEM((M, KP), BF),
            pltpu.VMEM((6, KP, F), BF),
            pltpu.VMEM((4, M, F), F32),
            pltpu.VMEM((M, F), F32),
            pltpu.VMEM((4, 2, steps, C, F), BF),
            pltpu.VMEM((4, 2, steps, C, F), BF),
            pltpu.VMEM((2, M, F), BF),
            pltpu.VMEM((2, M, F), BF),
            pltpu.VMEM((M, KP), F32),
            pltpu.VMEM((M, KP), BF),
            pltpu.VMEM((max(NT - 1, 1), R, KP), BF),
            pltpu.VMEM((M, KP), BF),
            pltpu.VMEM((R, KP), BF),
            pltpu.VMEM((NY - 1, R, KP), BF),
            pltpu.VMEM((NY, 2, KP), F32),
            pltpu.VMEM((3, KP, F), F32),
            *piece(FA),
            *piece(F - FA),
            pltpu.SemaphoreType.DMA((n_links,)),
            pltpu.SemaphoreType.DMA((n_links,)),
            pltpu.SemaphoreType.DMA((6,)),
        ],
        compiler_params=pltpu.CompilerParams(
            collective_id=0, has_side_effects=True, vmem_limit_bytes=62 * 1024 * 1024
        ),
    )(inputs, curvature, w_gate, w_up, v_gate, v_up, w_down.T, v_down.T)
    arrays = (to, pg, pu, pd)
    to, pg, pu, pd = pl.pallas_call(
        hand_on,
        out_shape=[jax.ShapeDtypeStruct(a.shape, a.dtype) for a in arrays],
        in_specs=[vmem] * 4,
        out_specs=[vmem] * 4,
    )(*arrays)
    return to, pg, pu, pd.T


def solution(mesh):
    ndp, nt = mesh.shape["dp"], mesh.shape["tensor"]
    return jax.shard_map(
        functools.partial(on_device, ndp // 4, nt),
        mesh=mesh,
        in_specs=(
            P(("dp", "tensor"), None),
            P(("dp", "tensor")),
            P("dp", "tensor"),
            P("dp", "tensor"),
            P("tensor", "dp"),
            P("dp", "tensor"),
            P("dp", "tensor"),
            P("tensor", "dp"),
        ),
        out_specs=(
            P(("dp", "tensor"), None),
            P("dp", "tensor"),
            P("dp", "tensor"),
            P("tensor", "dp"),
        ),
        check_vma=False,
    )
```

```python
import functools

import jax
import jax.numpy as jnp
from jax import lax
from jax.experimental import pallas as pl
from jax.experimental.pallas import tpu as pltpu
from jax.sharding import PartitionSpec as P

MESH = pl.DeviceIdType.MESH
BF = jnp.bfloat16
F32 = jnp.float32


def dot(a, b, ca, cb):
    return lax.dot_general(a, b, (((ca,), (cb,)), ((), ())), preferred_element_type=F32)


def first_piece(F):
    return (F // 2 + 127) // 128 * 128 if F > 256 else F // 2


class Link:
    def __init__(self, sems, slot, src, dst, device):
        self.copy = pltpu.make_async_remote_copy(
            src_ref=src,
            dst_ref=dst,
            send_sem=sems[0].at[slot],
            recv_sem=sems[1].at[slot],
            device_id=device,
            device_id_type=MESH,
        )
        self.copy.start()

    def arrive(self):
        self.copy.wait_recv()

    def left(self):
        self.copy.wait_send()


def kernel(
    NY, NT, D, F, KP,
    x_in, curv_in, wg, wu, vg, vu, wd, vd,
    to, pg, pu, pd,
    stage, xin, X, W, Pf, Pd, rs_s, rs_r, H, A,
    Tf, Tb, trecv, wt, osend, orecv, ot, PF,
    dh_sa, dh_ra, Ga, PBa, C1a, zsa, zra,
    dh_sb, dh_rb, Gb, PBb, C1b, zsb, zrb,
    send_sems, recv_sems, local_sems,
):
    K = 4 * D
    R = 2 * NY
    C = 2 * NT
    M = NT * R
    NX = 4 if NT % 4 == 0 else 1
    NH = NT // NX
    dp = lax.axis_index("dp")
    t = lax.axis_index("tensor")
    c = lax.rem(dp, 2)
    y = lax.rem(lax.div(dp, 2), NY)
    z = lax.div(dp, 2 * NY)

    def at(zz, yy, cc):
        return ((zz * NY + yy) * 2 + cc, t)

    core = at(z, y, 1 - c)
    zed = at(1 - z, y, c)

    def up_y(r):
        return lax.rem(y + r + NY, NY)

    def up_t(r):
        return lax.rem(t + r, NT)

    ypeers = [at(z, up_y(r), c) for r in range(1, NY)]
    tpeers = [(dp, up_t(r)) for r in range(1, NT)]
    xq, h = lax.rem(t, NX), lax.div(t, NX)

    def up_h(r):
        return lax.rem(h + r, NH) * NX + xq

    hpeers = [(dp, up_h(r)) for r in range(1, NH)]
    xpeers = [(dp, h * NX + lax.rem(xq + r, NX)) for r in range(1, NX)]

    barrier = pltpu.get_barrier_semaphore()
    peers = [core, zed] + ypeers + tpeers
    for peer in peers:
        pl.semaphore_signal(barrier, inc=1, device_id=peer, device_id_type=MESH)

    links = []
    count = [0]

    def send(src, dst, device):
        link = Link((send_sems, recv_sems), count[0], src, dst, device)
        count[0] += 1
        links.append(link)
        return link

    def rows(q):
        return pl.ds(pl.multiple_of(q * D, 16), D)

    def chunk(j, size):
        return pl.ds(pl.multiple_of(j * size, size), size)

    LT = KP // 128
    row = lax.broadcasted_iota(jnp.int32, (R, KP), 0)
    lane = lax.broadcasted_iota(jnp.int32, (2, KP), 1)
    packed = lax.broadcasted_iota(jnp.int32, (16, 128), 0)
    placed = lax.broadcasted_iota(jnp.int32, (R, 128), 0)
    raw = x_in[...].astype(F32)
    tail = lax.broadcasted_iota(jnp.int32, (2, KP - K), 0)
    tail = jnp.where(tail == 0, curv_in[0], curv_in[1])
    for j in range(NY):
        parts = [raw[:, (zz * NY + j) * 2 * D : (zz * NY + j + 1) * 2 * D] for zz in (0, 1)]
        a = jnp.concatenate(parts + [tail], axis=1)
        hi = a.astype(BF).astype(F32)
        mid = (a - hi).astype(BF).astype(F32)
        low = a - hi - mid
        a = jnp.where(lane == K + 1, mid, jnp.where(lane == K + 2, low, hi))
        block = jnp.zeros((16, 128), F32)
        for i in (0, 1):
            for m in range(LT):
                block = jnp.where(packed == i * LT + m, a[i : i + 1, m * 128 : (m + 1) * 128], block)
        stage[j] = block.astype(BF)
    pl.semaphore_wait(barrier, len(peers))

    y_order = sorted(range(1, NY), key=lambda r: abs(r - NY // 2))
    xa = {r - 1: send(stage.at[up_y(r)], xin.at[r - 1], ypeers[r - 1]) for r in y_order}

    own, other = z * 2 + c, (1 - z) * 2 + c
    mats = (wg, wu, vg, vu, wd, vd)
    locals_, from_core, from_z, forwards = {}, {}, {}, {}

    def fetch(k):
        dst = W.at[k, rows(own)]
        from_z[k] = send(mats[k], dst, zed)
        from_core[k] = send(mats[k], dst, core)
        locals_[k] = pltpu.make_async_copy(mats[k], dst, local_sems.at[k])
        locals_[k].start()

    def forward(k):
        from_z[k].arrive()
        forwards[k] = send(W.at[k, rows(other)], W.at[k, rows(other)], core)

    def have(k):
        locals_[k].wait()
        from_core[k].arrive()
        forwards[k].arrive()

    fetch(0)
    if KP > K:
        for k in range(6):
            W[k, K:KP, :] = jnp.zeros((KP - K, F), BF)

    x16 = [jnp.zeros((R, 128), F32)] * LT
    for r in [0] + y_order[::-1]:
        if r:
            xa[r - 1].arrive()
        block = (xin[r - 1] if r else stage[y]).astype(F32)
        for i in (0, 1):
            here = placed == 2 * up_y(-r) + i
            for m in range(LT):
                x16[m] = jnp.where(here, block[i * LT + m : i * LT + m + 1], x16[m])
    x16 = jnp.concatenate(x16, axis=1)
    curv = x16[:, K : K + 1] + x16[:, K + 1 : K + 2] + x16[:, K + 2 : K + 3]
    X[chunk(t, R)] = x16.astype(BF)

    def all_tensor(buf):
        h_order = sorted(range(1, NH), key=lambda r: abs(r - NH // 2))
        got = {r: send(buf.at[chunk(t, R)], buf.at[chunk(t, R)], hpeers[r - 1]) for r in h_order}

        def second():
            block = {}
            mine = [buf.at[chunk(t, R)]] + [buf.at[chunk(up_h(r), R)] for r in range(1, NH)]
            for n in [0] + h_order[::-1]:
                ref = mine[n]
                if n:
                    got[NH - n].arrive()
                for p in xpeers:
                    block[n, len(block)] = send(ref, ref, p)
            return list(block.values())

        return second

    second = all_tensor(X)
    fetch(1)
    xg = second()
    fetch(2)
    fetch(3)
    forward(0)
    forward(1)
    for link in xg:
        link.arrive()
    x = X[...]

    def dist(d, n):
        return at(z, up_y(d * n), c)

    def reach(k, d):
        return NY // 2 - (1 if (k % 2 == 0) == (d > 0) else 0)

    def reduce_ring(k, part, sent, recv, b=None):
        got = {}
        b = k if b is None else b

        def step(s):
            for i, d in enumerate((-1, 1)):
                n = reach(k, d)
                if s > n:
                    continue
                v = part(k, up_y(d * (n - s + 1)))
                if s > 1:
                    got[i].arrive()
                    v = v + recv[b, i, s - 2].astype(F32)
                sent[b, i, s - 1] = v.astype(BF)
                got[i] = send(sent.at[b, i, s - 1], recv.at[b, i, s - 1], dist(d, 1))

        def total():
            v = part(k, y)
            for i, d in enumerate((-1, 1)):
                if reach(k, d):
                    got[i].arrive()
                    v = v + recv[b, i, reach(k, d) - 1].astype(F32)
            return v

        return {s: functools.partial(step, s) for s in range(1, NY // 2 + 1)}, total

    def reduce_tree(k, part, sent, recv, b=None):
        got = {}
        b = k if b is None else b

        def push(i, d, slot, v, far):
            sent[b, i, slot] = v.astype(BF)
            got[i, slot] = send(sent.at[b, i, slot], recv.at[b, i, slot], dist(d, far))

        def first():
            for i, d in enumerate((-1, 1)):
                if reach(k, d) == 4:
                    push(i, d, 0, part(k, up_y(4 * d)), 2)
                push(i, d, 1, part(k, up_y(3 * d)), 1)
            for i, d in enumerate((-1, 1)):
                push(i, d, 2, part(k, up_y(d)), 1)

        def second():
            for i, d in enumerate((-1, 1)):
                v = part(k, up_y(2 * d))
                for slot in (1, 0) if reach(k, d) == 4 else (1,):
                    got[i, slot].arrive()
                    v = v + recv[b, i, slot].astype(F32)
                push(i, d, 3, v, 2)

        def total():
            v = part(k, y)
            for slot in (2, 3):
                for i in (0, 1):
                    got[i, slot].arrive()
                    v = v + recv[b, i, slot].astype(F32)
            return v

        return {1: first, 2: second}, total

    def gather_ring(k, ref):
        got = {}

        def step(s):
            for i, d in enumerate((-1, 1)):
                if s > reach(k, d):
                    continue
                if s > 1:
                    got[i].arrive()
                block = ref(up_y(-d * (s - 1)))
                got[i] = send(block, block, dist(d, 1))

        def finish():
            for i in got:
                got[i].arrive()

        return {s: functools.partial(step, s) for s in range(1, NY // 2 + 1)}, finish

    def gather_tree(k, ref):
        got = {}

        def first():
            for far in (2, 1):
                for i, d in enumerate((-1, 1)):
                    got[i, 2 - far] = send(ref(y), ref(y), dist(d, far))

        def second():
            for i, d in enumerate((-1, 1)):
                got[i, 0].arrive()
                block = ref(up_y(-2 * d))
                if reach(k, d) == 4:
                    got[i, 3] = send(block, block, dist(d, 2))
                got[i, 2] = send(block, block, dist(d, 1))

        def finish():
            for i, slot in got:
                if slot:
                    got[i, slot].arrive()

        return {1: first, 2: second}, finish

    def in_waves(plans, late=None, between=None):
        steps = []
        for n, (waves, _) in enumerate(plans):
            steps += [(w + (late[n] if late else 0), n, f) for w, f in waves.items()]
        last = None
        for w, n, f in sorted(steps, key=lambda e: e[:2]):
            if between and last is not None and w != last and last in between:
                between[last]()
            last = w
            f()

    if NY != 8:
        reduce_tree, gather_tree = reduce_ring, gather_ring

    def part(k, j):
        return Pf[k, chunk(j, C)]

    def begin(k):
        if k >= 2:
            forward(k)
        have(k)
        Pf[k] = dot(x, W[k], 1, 0)

    plans = []
    for k in range(4):
        waves, total = reduce_ring(k, part, rs_s, rs_r)

        def opened(k=k, step=waves[1]):
            begin(k)
            step()

        waves[1] = opened
        plans.append((waves, total))

    def down():
        fetch(4)
        fetch(5)

    in_waves(plans, None, {1: down} if NY > 2 else None)
    if NY == 2:
        down()
    half = C // 2

    def piece(buf, n, q):
        return lambda j: buf.at[n, pl.ds(pl.multiple_of(j * C + q * half, half), half)]

    def steps_of(pair, w):
        for waves, _ in pair:
            if w in waves:
                waves[w]()

    gate, up = plans[0][1](), plans[1][1]()
    sig = jax.nn.sigmoid(gate)
    act = gate * sig
    slope = sig * (1.0 + gate * (1.0 - sig))
    up_slope = up * slope
    H[0, chunk(y, C)] = (act * up).astype(BF)
    hid = [gather_tree(q, piece(H, 0, q)) for q in (0, 1)]
    steps_of(hid, 1)
    A[0, chunk(y, C)] = act.astype(BF)
    A[1, chunk(y, C)] = up_slope.astype(BF)
    dgate, dup = plans[2][1](), plans[3][1]()
    H[1, chunk(y, C)] = (up_slope * dgate + act * dup).astype(BF)
    thid = [gather_tree(q, piece(H, 1, q)) for q in (0, 1)]
    steps_of(thid, 1)
    for w in range(2, NY // 2 + 1):
        steps_of(hid, w)
        steps_of(thid, w)
    plans = hid + thid
    forward(4)
    forward(5)
    have(4)
    have(5)
    plans[0][1]()
    plans[1][1]()
    tangent = dot(H[0], W[5], 1, 1)
    plans[2][1]()
    plans[3][1]()
    tangent = tangent + dot(H[1], W[4], 1, 1)

    Tf[...] = tangent
    Tb[...] = tangent.astype(BF)
    far_first = sorted(range(1, NT), key=lambda r: abs(r - NT // 2))
    tr = {r - 1: send(Tb.at[chunk(up_t(r), R)], trecv.at[r - 1], tpeers[r - 1]) for r in far_first}
    aplans = [gather_tree(n, lambda j, n=n: A.at[n, chunk(j, C)]) for n in (0, 1)]
    aplans[0][0][1]()
    aplans[1][0][1]()
    total = Tf[chunk(t, R)]
    for r in range(1, NT):
        tr[r - 1].arrive()
        total = total + trecv[r - 1].astype(F32)
    wt[chunk(t, R)] = (curv * total).astype(BF)
    tw = [send(wt.at[chunk(t, R)], wt.at[chunk(t, R)], tpeers[r - 1]) for r in far_first]
    osend[...] = total.astype(BF)
    oa = [send(osend, orecv.at[r - 1], ypeers[r - 1]) for r in range(1, NY)]
    for w in sorted(aplans[0][0])[1:]:
        aplans[0][0][w]()
        aplans[1][0][w]()
    for link in tw:
        link.arrive()
    weighted = wt[...]

    Pd[...] = dot(weighted, W[4], 1, 0)

    FA = first_piece(F)
    lanes = (slice(0, FA), slice(FA, F))
    dh_s, dh_r, G = (dh_sa, dh_sb), (dh_ra, dh_rb), (Ga, Gb)
    PB, C1, zs, zr = (PBa, PBb), (C1a, C1b), (zsa, zsb), (zra, zrb)

    stage1, stage2 = {}, {}

    def product(i, q, lhs, rhs):
        full = dot(lhs, rhs, 0, 0)
        PF[i, :, lanes[q]] = full
        PB[q][i] = full.astype(BF)
        for n, zz in enumerate((1 - z, z)):
            stage1[i, q, n] = send(PB[q].at[i, rows(zz * 2 + 1 - c)], C1[q].at[i, n], core)

    def cross(i, q):
        stage1[i, q, 0].arrive()
        zs[q][i] = (PF[i, rows((1 - z) * 2 + c), lanes[q]] + C1[q][i, 0].astype(F32)).astype(BF)
        stage2[i, q] = send(zs[q].at[i], zr[q].at[i], zed)

    def settle(i, q, out):
        stage1[i, q, 1].arrive()
        mine = PF[i, rows(z * 2 + c), lanes[q]] + C1[q][i, 1].astype(F32)
        stage2[i, q].arrive()
        out[:, lanes[q]] = mine + zr[q][i].astype(F32)

    def part_of(k, j):
        return Pd[chunk(j, C), lanes[k]]

    sums = [reduce_tree(k, part_of, dh_s[k], dh_r[k], 0) for k in (0, 1)]
    steps_of(sums, 1)
    for q in (0, 1):
        product(2, q, weighted, H[0, :, lanes[q]])
    for w in range(2, NY // 2 + 1):
        steps_of(sums, w)
    back = []
    for k in (0, 1):
        G[k][chunk(y, C)] = sums[k][1]().astype(BF)
        back.append(gather_tree(k, lambda j, k=k: G[k].at[chunk(j, C)]))
        steps_of(back[k:], 1)
    for q in (0, 1):
        cross(2, q)
    for _, finish in aplans:
        finish()

    def two_rows(v):
        v = v.astype(F32)
        return [jnp.sum(jnp.where(row == 2 * y + i, v, 0.0), axis=0, keepdims=True) for i in (0, 1)]

    for r in range(NY):
        if r:
            oa[r - 1].arrive()
        a, b = two_rows(orecv[r - 1] if r else osend[...])
        ot[up_y(-r)] = jnp.concatenate([a, b], axis=0)
    for w in range(2, NY // 2 + 1):
        steps_of(back, w)
    for j in range(NY):
        v = ot[j].astype(BF)
        for zz in (0, 1):
            to[:, (zz * NY + j) * 2 * D : (zz * NY + j + 1) * 2 * D] = v[:, zz * 2 * D : (zz + 1) * 2 * D]

    for q in (0, 1):
        back[q][1]()
        dhid = G[q][...].astype(F32)
        product(0, q, x, (dhid * A[1, :, lanes[q]].astype(F32)).astype(BF))
        bup = (dhid * A[0, :, lanes[q]].astype(F32)).astype(BF)
        cross(0, q)
        product(1, q, x, bup)
        cross(1, q)
    for q in (0, 1):
        settle(2, q, pd)
        settle(0, q, pg)
        settle(1, q, pu)
    for link in links:
        link.left()


def hand_on(*refs):
    for i in range(4):
        refs[4 + i][...] = refs[i][...]


def on_device(NY, NT, inputs, curvature, w_gate, w_up, w_down, v_gate, v_up, v_down):
    D, F = w_gate.shape
    K = 4 * D
    KP = -(-(K + 3) // 128) * 128
    R, C = 2 * NY, 2 * NT
    M = NT * R
    steps = NY // 2
    FA = first_piece(F)

    def piece(n):
        return [
            pltpu.VMEM((1, 2, steps, C, n), BF),
            pltpu.VMEM((1, 2, steps, C, n), BF),
            pltpu.VMEM((M, n), BF),
            pltpu.VMEM((3, KP, n), BF),
            pltpu.VMEM((3, 2, D, n), BF),
            pltpu.VMEM((3, D, n), BF),
            pltpu.VMEM((3, D, n), BF),
        ]

    n_links = 2 * (NY - 1) + 3 * (NT - 1) + 18 + 18 + 14 * (NY - 1)
    vmem = pl.BlockSpec(memory_space=pltpu.VMEM)
    hbm = pl.BlockSpec(memory_space=pl.ANY)
    to, pg, pu, pd = pl.pallas_call(
        functools.partial(kernel, NY, NT, D, F, KP),
        out_shape=[
            jax.ShapeDtypeStruct((2, 4 * NY * D), BF),
            jax.ShapeDtypeStruct((D, F), F32),
            jax.ShapeDtypeStruct((D, F), F32),
            jax.ShapeDtypeStruct((D, F), F32),
        ],
        in_specs=[vmem, pl.BlockSpec(memory_space=pltpu.SMEM)] + [hbm] * 6,
        out_specs=[vmem] * 4,
        scratch_shapes=[
            pltpu.VMEM((NY, 16, 128), BF),
            pltpu.VMEM((NY - 1, 16, 128), BF),
            pltpu.VMEM((M, KP), BF),
            pltpu.VMEM((6, KP, F), BF),
            pltpu.VMEM((4, M, F), F32),
            pltpu.VMEM((M, F), F32),
            pltpu.VMEM((4, 2, steps, C, F), BF),
            pltpu.VMEM((4, 2, steps, C, F), BF),
            pltpu.VMEM((2, M, F), BF),
            pltpu.VMEM((2, M, F), BF),
            pltpu.VMEM((M, KP), F32),
            pltpu.VMEM((M, KP), BF),
            pltpu.VMEM((max(NT - 1, 1), R, KP), BF),
            pltpu.VMEM((M, KP), BF),
            pltpu.VMEM((R, KP), BF),
            pltpu.VMEM((NY - 1, R, KP), BF),
            pltpu.VMEM((NY, 2, KP), F32),
            pltpu.VMEM((3, KP, F), F32),
            *piece(FA),
            *piece(F - FA),
            pltpu.SemaphoreType.DMA((n_links,)),
            pltpu.SemaphoreType.DMA((n_links,)),
            pltpu.SemaphoreType.DMA((6,)),
        ],
        compiler_params=pltpu.CompilerParams(
            collective_id=0, has_side_effects=True, vmem_limit_bytes=62 * 1024 * 1024
        ),
    )(inputs, curvature, w_gate, w_up, v_gate, v_up, w_down.T, v_down.T)
    arrays = (to, pg, pu, pd)
    to, pg, pu, pd = pl.pallas_call(
        hand_on,
        out_shape=[jax.ShapeDtypeStruct(a.shape, a.dtype) for a in arrays],
        in_specs=[vmem] * 4,
        out_specs=[vmem] * 4,
    )(*arrays)
    return to, pg, pu, pd.T


def solution(mesh):
    ndp, nt = mesh.shape["dp"], mesh.shape["tensor"]
    return jax.shard_map(
        functools.partial(on_device, ndp // 4, nt),
        mesh=mesh,
        in_specs=(
            P(("dp", "tensor"), None),
            P(("dp", "tensor")),
            P("dp", "tensor"),
            P("dp", "tensor"),
            P("tensor", "dp"),
            P("dp", "tensor"),
            P("dp", "tensor"),
            P("tensor", "dp"),
        ),
        out_specs=(
            P(("dp", "tensor"), None),
            P("dp", "tensor"),
            P("dp", "tensor"),
            P("tensor", "dp"),
        ),
        check_vma=False,
    )
```

```python
import functools

import jax
import jax.numpy as jnp
from jax import lax
from jax.experimental import pallas as pl
from jax.experimental.pallas import tpu as pltpu
from jax.sharding import PartitionSpec as P

MESH = pl.DeviceIdType.MESH
BF = jnp.bfloat16
F32 = jnp.float32


def dot(a, b, ca, cb):
    return lax.dot_general(a, b, (((ca,), (cb,)), ((), ())), preferred_element_type=F32)


def first_piece(F):
    return F // 256 * 128 if F > 256 else F // 2


class Link:
    def __init__(self, sems, slot, src, dst, device):
        self.copy = pltpu.make_async_remote_copy(
            src_ref=src,
            dst_ref=dst,
            send_sem=sems[0].at[slot],
            recv_sem=sems[1].at[slot],
            device_id=device,
            device_id_type=MESH,
        )
        self.copy.start()

    def arrive(self):
        self.copy.wait_recv()

    def left(self):
        self.copy.wait_send()


def kernel(
    NY, NT, D, F, KP,
    x_in, curv_in, wg, wu, vg, vu, wd, vd,
    to, pg, pu, pd,
    stage, xin, X, W, Pf, Pd, rs_s, rs_r, H, A,
    Tf, Tb, trecv, wt, osend, orecv, ot, PF,
    dh_sa, dh_ra, Ga, PBa, C1a, zsa, zra,
    dh_sb, dh_rb, Gb, PBb, C1b, zsb, zrb,
    send_sems, recv_sems, local_sems,
):
    K = 4 * D
    R = 2 * NY
    C = 2 * NT
    M = NT * R
    NX = 4 if NT % 4 == 0 else 1
    NH = NT // NX
    dp = lax.axis_index("dp")
    t = lax.axis_index("tensor")
    c = lax.rem(dp, 2)
    y = lax.rem(lax.div(dp, 2), NY)
    z = lax.div(dp, 2 * NY)

    def at(zz, yy, cc):
        return ((zz * NY + yy) * 2 + cc, t)

    core = at(z, y, 1 - c)
    zed = at(1 - z, y, c)

    def up_y(r):
        return lax.rem(y + r + NY, NY)

    def up_t(r):
        return lax.rem(t + r, NT)

    ypeers = [at(z, up_y(r), c) for r in range(1, NY)]
    tpeers = [(dp, up_t(r)) for r in range(1, NT)]
    xq, h = lax.rem(t, NX), lax.div(t, NX)

    def up_h(r):
        return lax.rem(h + r, NH) * NX + xq

    hpeers = [(dp, up_h(r)) for r in range(1, NH)]
    xpeers = [(dp, h * NX + lax.rem(xq + r, NX)) for r in range(1, NX)]

    barrier = pltpu.get_barrier_semaphore()
    peers = [core, zed] + ypeers + tpeers
    for peer in peers:
        pl.semaphore_signal(barrier, inc=1, device_id=peer, device_id_type=MESH)

    links = []
    count = [0]

    def send(src, dst, device):
        link = Link((send_sems, recv_sems), count[0], src, dst, device)
        count[0] += 1
        links.append(link)
        return link

    def rows(q):
        return pl.ds(pl.multiple_of(q * D, 16), D)

    def chunk(j, size):
        return pl.ds(pl.multiple_of(j * size, size), size)

    LT = KP // 128
    row = lax.broadcasted_iota(jnp.int32, (R, KP), 0)
    lane = lax.broadcasted_iota(jnp.int32, (2, KP), 1)
    packed = lax.broadcasted_iota(jnp.int32, (16, 128), 0)
    placed = lax.broadcasted_iota(jnp.int32, (R, 128), 0)
    raw = x_in[...].astype(F32)
    tail = lax.broadcasted_iota(jnp.int32, (2, KP - K), 0)
    tail = jnp.where(tail == 0, curv_in[0], curv_in[1])
    for j in range(NY):
        parts = [raw[:, (zz * NY + j) * 2 * D : (zz * NY + j + 1) * 2 * D] for zz in (0, 1)]
        a = jnp.concatenate(parts + [tail], axis=1)
        hi = a.astype(BF).astype(F32)
        mid = (a - hi).astype(BF).astype(F32)
        low = a - hi - mid
        a = jnp.where(lane == K + 1, mid, jnp.where(lane == K + 2, low, hi))
        block = jnp.zeros((16, 128), F32)
        for i in (0, 1):
            for m in range(LT):
                block = jnp.where(packed == i * LT + m, a[i : i + 1, m * 128 : (m + 1) * 128], block)
        stage[j] = block.astype(BF)
    pl.semaphore_wait(barrier, len(peers))

    y_order = sorted(range(1, NY), key=lambda r: abs(r - NY // 2))
    xa = {r - 1: send(stage.at[up_y(r)], xin.at[r - 1], ypeers[r - 1]) for r in y_order}

    own, other = z * 2 + c, (1 - z) * 2 + c
    mats = (wg, wu, vg, vu, wd, vd)
    locals_, from_core, from_z, forwards = {}, {}, {}, {}

    def fetch(k):
        dst = W.at[k, rows(own)]
        from_z[k] = send(mats[k], dst, zed)
        from_core[k] = send(mats[k], dst, core)
        locals_[k] = pltpu.make_async_copy(mats[k], dst, local_sems.at[k])
        locals_[k].start()

    def forward(k):
        from_z[k].arrive()
        forwards[k] = send(W.at[k, rows(other)], W.at[k, rows(other)], core)

    def have(k):
        locals_[k].wait()
        from_core[k].arrive()
        forwards[k].arrive()

    fetch(0)
    if KP > K:
        for k in range(6):
            W[k, K:KP, :] = jnp.zeros((KP - K, F), BF)

    x16 = [jnp.zeros((R, 128), F32)] * LT
    for r in [0] + y_order[::-1]:
        if r:
            xa[r - 1].arrive()
        block = (xin[r - 1] if r else stage[y]).astype(F32)
        for i in (0, 1):
            here = placed == 2 * up_y(-r) + i
            for m in range(LT):
                x16[m] = jnp.where(here, block[i * LT + m : i * LT + m + 1], x16[m])
    x16 = jnp.concatenate(x16, axis=1)
    curv = x16[:, K : K + 1] + x16[:, K + 1 : K + 2] + x16[:, K + 2 : K + 3]
    X[chunk(t, R)] = x16.astype(BF)

    def all_tensor(buf):
        h_order = sorted(range(1, NH), key=lambda r: abs(r - NH // 2))
        got = {r: send(buf.at[chunk(t, R)], buf.at[chunk(t, R)], hpeers[r - 1]) for r in h_order}

        def second():
            block = {}
            mine = [buf.at[chunk(t, R)]] + [buf.at[chunk(up_h(r), R)] for r in range(1, NH)]
            for n in [0] + h_order[::-1]:
                ref = mine[n]
                if n:
                    got[NH - n].arrive()
                for p in xpeers:
                    block[n, len(block)] = send(ref, ref, p)
            return list(block.values())

        return second

    second = all_tensor(X)
    fetch(1)
    xg = second()
    fetch(2)
    fetch(3)
    forward(0)
    forward(1)
    for link in xg:
        link.arrive()
    x = X[...]

    def dist(d, n):
        return at(z, up_y(d * n), c)

    def reach(k, d):
        return NY // 2 - (1 if (k % 2 == 0) == (d > 0) else 0)

    def reduce_ring(k, part, sent, recv, b=None):
        got = {}
        b = k if b is None else b

        def step(s):
            for i, d in enumerate((-1, 1)):
                n = reach(k, d)
                if s > n:
                    continue
                v = part(k, up_y(d * (n - s + 1)))
                if s > 1:
                    got[i].arrive()
                    v = v + recv[b, i, s - 2].astype(F32)
                sent[b, i, s - 1] = v.astype(BF)
                got[i] = send(sent.at[b, i, s - 1], recv.at[b, i, s - 1], dist(d, 1))

        def total():
            v = part(k, y)
            for i, d in enumerate((-1, 1)):
                if reach(k, d):
                    got[i].arrive()
                    v = v + recv[b, i, reach(k, d) - 1].astype(F32)
            return v

        return {s: functools.partial(step, s) for s in range(1, NY // 2 + 1)}, total

    def reduce_tree(k, part, sent, recv, b=None):
        got = {}
        b = k if b is None else b

        def push(i, d, slot, v, far):
            sent[b, i, slot] = v.astype(BF)
            got[i, slot] = send(sent.at[b, i, slot], recv.at[b, i, slot], dist(d, far))

        def first():
            for i, d in enumerate((-1, 1)):
                if reach(k, d) == 4:
                    push(i, d, 0, part(k, up_y(4 * d)), 2)
                push(i, d, 1, part(k, up_y(3 * d)), 1)
            for i, d in enumerate((-1, 1)):
                push(i, d, 2, part(k, up_y(d)), 1)

        def second():
            for i, d in enumerate((-1, 1)):
                v = part(k, up_y(2 * d))
                for slot in (1, 0) if reach(k, d) == 4 else (1,):
                    got[i, slot].arrive()
                    v = v + recv[b, i, slot].astype(F32)
                push(i, d, 3, v, 2)

        def total():
            v = part(k, y)
            for slot in (2, 3):
                for i in (0, 1):
                    got[i, slot].arrive()
                    v = v + recv[b, i, slot].astype(F32)
            return v

        return {1: first, 2: second}, total

    def gather_ring(k, ref):
        got = {}

        def step(s):
            for i, d in enumerate((-1, 1)):
                if s > reach(k, d):
                    continue
                if s > 1:
                    got[i].arrive()
                block = ref(up_y(-d * (s - 1)))
                got[i] = send(block, block, dist(d, 1))

        def finish():
            for i in got:
                got[i].arrive()

        return {s: functools.partial(step, s) for s in range(1, NY // 2 + 1)}, finish

    def gather_tree(k, ref):
        got = {}

        def first():
            for far in (2, 1):
                for i, d in enumerate((-1, 1)):
                    got[i, 2 - far] = send(ref(y), ref(y), dist(d, far))

        def second():
            for i, d in enumerate((-1, 1)):
                got[i, 0].arrive()
                block = ref(up_y(-2 * d))
                if reach(k, d) == 4:
                    got[i, 3] = send(block, block, dist(d, 2))
                got[i, 2] = send(block, block, dist(d, 1))

        def finish():
            for i, slot in got:
                if slot:
                    got[i, slot].arrive()

        return {1: first, 2: second}, finish

    def in_waves(plans, late=None, between=None):
        steps = []
        for n, (waves, _) in enumerate(plans):
            steps += [(w + (late[n] if late else 0), n, f) for w, f in waves.items()]
        last = None
        for w, n, f in sorted(steps, key=lambda e: e[:2]):
            if between and last is not None and w != last and last in between:
                between[last]()
            last = w
            f()

    if NY != 8:
        reduce_tree, gather_tree = reduce_ring, gather_ring

    def part(k, j):
        return Pf[k, chunk(j, C)]

    def begin(k):
        if k >= 2:
            forward(k)
        have(k)
        Pf[k] = dot(x, W[k], 1, 0)

    plans = []
    for k in range(4):
        waves, total = reduce_ring(k, part, rs_s, rs_r)

        def opened(k=k, step=waves[1]):
            begin(k)
            step()

        waves[1] = opened
        plans.append((waves, total))

    def down():
        fetch(4)
        fetch(5)

    in_waves(plans, None, {1: down} if NY > 2 else None)
    if NY == 2:
        down()
    def steps_of(pair, w):
        for waves, _ in pair:
            if w in waves:
                waves[w]()

    gate, up = plans[0][1](), plans[1][1]()
    sig = jax.nn.sigmoid(gate)
    act = gate * sig
    slope = sig * (1.0 + gate * (1.0 - sig))
    up_slope = up * slope
    H[0, chunk(y, C)] = (act * up).astype(BF)
    hid = [gather_tree(0, lambda j: H.at[0, chunk(j, C)])]
    steps_of(hid, 1)
    A[0, chunk(y, C)] = act.astype(BF)
    A[1, chunk(y, C)] = up_slope.astype(BF)
    dgate, dup = plans[2][1](), plans[3][1]()
    H[1, chunk(y, C)] = (up_slope * dgate + act * dup).astype(BF)
    thid = [gather_tree(1, lambda j: H.at[1, chunk(j, C)])]
    steps_of(thid, 1)
    for w in range(2, NY // 2 + 1):
        steps_of(hid, w)
        steps_of(thid, w)
    plans = hid + thid
    forward(4)
    forward(5)
    have(4)
    have(5)
    plans[0][1]()
    tangent = dot(H[0], W[5], 1, 1)
    plans[1][1]()
    tangent = tangent + dot(H[1], W[4], 1, 1)

    Tf[...] = tangent
    Tb[...] = tangent.astype(BF)
    far_first = sorted(range(1, NT), key=lambda r: abs(r - NT // 2))
    tr = {r - 1: send(Tb.at[chunk(up_t(r), R)], trecv.at[r - 1], tpeers[r - 1]) for r in far_first}
    aplans = [gather_tree(n, lambda j, n=n: A.at[n, chunk(j, C)]) for n in (0, 1)]
    aplans[0][0][1]()
    aplans[1][0][1]()
    total = Tf[chunk(t, R)]
    for r in range(1, NT):
        tr[r - 1].arrive()
        total = total + trecv[r - 1].astype(F32)
    wt[chunk(t, R)] = (curv * total).astype(BF)
    tw = [send(wt.at[chunk(t, R)], wt.at[chunk(t, R)], tpeers[r - 1]) for r in far_first]
    osend[...] = total.astype(BF)
    oa = [send(osend, orecv.at[r - 1], ypeers[r - 1]) for r in range(1, NY)]
    for w in sorted(aplans[0][0])[1:]:
        aplans[0][0][w]()
        aplans[1][0][w]()
    for link in tw:
        link.arrive()
    weighted = wt[...]

    Pd[...] = dot(weighted, W[4], 1, 0)

    FA = first_piece(F)
    lanes = (slice(0, FA), slice(FA, F))
    dh_s, dh_r, G = (dh_sa, dh_sb), (dh_ra, dh_rb), (Ga, Gb)
    PB, C1, zs, zr = (PBa, PBb), (C1a, C1b), (zsa, zsb), (zra, zrb)

    stage1, stage2 = {}, {}

    def product(i, q, lhs, rhs):
        full = dot(lhs, rhs, 0, 0)
        PF[i, :, lanes[q]] = full
        PB[q][i] = full.astype(BF)
        for n, zz in enumerate((1 - z, z)):
            stage1[i, q, n] = send(PB[q].at[i, rows(zz * 2 + 1 - c)], C1[q].at[i, n], core)

    def cross(i, q):
        stage1[i, q, 0].arrive()
        zs[q][i] = (PF[i, rows((1 - z) * 2 + c), lanes[q]] + C1[q][i, 0].astype(F32)).astype(BF)
        stage2[i, q] = send(zs[q].at[i], zr[q].at[i], zed)

    def settle(i, q, out):
        stage1[i, q, 1].arrive()
        mine = PF[i, rows(z * 2 + c), lanes[q]] + C1[q][i, 1].astype(F32)
        stage2[i, q].arrive()
        out[:, lanes[q]] = mine + zr[q][i].astype(F32)

    def part_of(k, j):
        return Pd[chunk(j, C), lanes[k]]

    sums = [reduce_tree(k, part_of, dh_s[k], dh_r[k], 0) for k in (0, 1)]
    steps_of(sums, 1)
    for q in (0, 1):
        product(2, q, weighted, H[0, :, lanes[q]])
    for w in range(2, NY // 2 + 1):
        steps_of(sums, w)
    back = []
    for k in (0, 1):
        G[k][chunk(y, C)] = sums[k][1]().astype(BF)
        back.append(gather_tree(k, lambda j, k=k: G[k].at[chunk(j, C)]))
        steps_of(back[k:], 1)
    for q in (0, 1):
        cross(2, q)
    for _, finish in aplans:
        finish()

    def two_rows(v):
        v = v.astype(F32)
        return [jnp.sum(jnp.where(row == 2 * y + i, v, 0.0), axis=0, keepdims=True) for i in (0, 1)]

    for r in range(NY):
        if r:
            oa[r - 1].arrive()
        a, b = two_rows(orecv[r - 1] if r else osend[...])
        ot[up_y(-r)] = jnp.concatenate([a, b], axis=0)
    for w in range(2, NY // 2 + 1):
        steps_of(back, w)
    for j in range(NY):
        v = ot[j].astype(BF)
        for zz in (0, 1):
            to[:, (zz * NY + j) * 2 * D : (zz * NY + j + 1) * 2 * D] = v[:, zz * 2 * D : (zz + 1) * 2 * D]

    for q in (0, 1):
        back[q][1]()
        dhid = G[q][...].astype(F32)
        product(0, q, x, (dhid * A[1, :, lanes[q]].astype(F32)).astype(BF))
        bup = (dhid * A[0, :, lanes[q]].astype(F32)).astype(BF)
        cross(0, q)
        product(1, q, x, bup)
        cross(1, q)
    for q in (0, 1):
        settle(2, q, pd)
        settle(0, q, pg)
        settle(1, q, pu)
    for link in links:
        link.left()


def hand_on(*refs):
    for i in range(4):
        refs[4 + i][...] = refs[i][...]


def on_device(NY, NT, inputs, curvature, w_gate, w_up, w_down, v_gate, v_up, v_down):
    D, F = w_gate.shape
    K = 4 * D
    KP = -(-(K + 3) // 128) * 128
    R, C = 2 * NY, 2 * NT
    M = NT * R
    steps = NY // 2
    FA = first_piece(F)

    def piece(n):
        return [
            pltpu.VMEM((1, 2, steps, C, n), BF),
            pltpu.VMEM((1, 2, steps, C, n), BF),
            pltpu.VMEM((M, n), BF),
            pltpu.VMEM((3, KP, n), BF),
            pltpu.VMEM((3, 2, D, n), BF),
            pltpu.VMEM((3, D, n), BF),
            pltpu.VMEM((3, D, n), BF),
        ]

    n_links = 2 * (NY - 1) + 3 * (NT - 1) + 18 + 18 + 14 * (NY - 1)
    vmem = pl.BlockSpec(memory_space=pltpu.VMEM)
    hbm = pl.BlockSpec(memory_space=pl.ANY)
    to, pg, pu, pd = pl.pallas_call(
        functools.partial(kernel, NY, NT, D, F, KP),
        out_shape=[
            jax.ShapeDtypeStruct((2, 4 * NY * D), BF),
            jax.ShapeDtypeStruct((D, F), F32),
            jax.ShapeDtypeStruct((D, F), F32),
            jax.ShapeDtypeStruct((D, F), F32),
        ],
        in_specs=[vmem, pl.BlockSpec(memory_space=pltpu.SMEM)] + [hbm] * 6,
        out_specs=[vmem] * 4,
        scratch_shapes=[
            pltpu.VMEM((NY, 16, 128), BF),
            pltpu.VMEM((NY - 1, 16, 128), BF),
            pltpu.VMEM((M, KP), BF),
            pltpu.VMEM((6, KP, F), BF),
            pltpu.VMEM((4, M, F), F32),
            pltpu.VMEM((M, F), F32),
            pltpu.VMEM((4, 2, steps, C, F), BF),
            pltpu.VMEM((4, 2, steps, C, F), BF),
            pltpu.VMEM((2, M, F), BF),
            pltpu.VMEM((2, M, F), BF),
            pltpu.VMEM((M, KP), F32),
            pltpu.VMEM((M, KP), BF),
            pltpu.VMEM((max(NT - 1, 1), R, KP), BF),
            pltpu.VMEM((M, KP), BF),
            pltpu.VMEM((R, KP), BF),
            pltpu.VMEM((NY - 1, R, KP), BF),
            pltpu.VMEM((NY, 2, KP), F32),
            pltpu.VMEM((3, KP, F), F32),
            *piece(FA),
            *piece(F - FA),
            pltpu.SemaphoreType.DMA((n_links,)),
            pltpu.SemaphoreType.DMA((n_links,)),
            pltpu.SemaphoreType.DMA((6,)),
        ],
        compiler_params=pltpu.CompilerParams(
            collective_id=0, has_side_effects=True, vmem_limit_bytes=62 * 1024 * 1024
        ),
    )(inputs, curvature, w_gate, w_up, v_gate, v_up, w_down.T, v_down.T)
    arrays = (to, pg, pu, pd)
    to, pg, pu, pd = pl.pallas_call(
        hand_on,
        out_shape=[jax.ShapeDtypeStruct(a.shape, a.dtype) for a in arrays],
        in_specs=[vmem] * 4,
        out_specs=[vmem] * 4,
    )(*arrays)
    return to, pg, pu, pd.T


def solution(mesh):
    ndp, nt = mesh.shape["dp"], mesh.shape["tensor"]
    return jax.shard_map(
        functools.partial(on_device, ndp // 4, nt),
        mesh=mesh,
        in_specs=(
            P(("dp", "tensor"), None),
            P(("dp", "tensor")),
            P("dp", "tensor"),
            P("dp", "tensor"),
            P("tensor", "dp"),
            P("dp", "tensor"),
            P("dp", "tensor"),
            P("tensor", "dp"),
        ),
        out_specs=(
            P(("dp", "tensor"), None),
            P("dp", "tensor"),
            P("dp", "tensor"),
            P("tensor", "dp"),
        ),
        check_vma=False,
    )
```
